32 devices in a mesh: req: 8 (over z, x), tile: 4 (over y, core).
Axes of the slice: x: 2, y: 2, z: 4, core: 2. Of those that a mesh axis runs over, the one named last changes fastest.
Arguments:
- latents: bfloat16 [256, 16, 128], P(('req', 'tile')), may hold values from -6 to 6
- piece_dest: int32 [256], replicated, may hold values from 0 to 255, as said below
- frames: int32 [8], replicated, may hold values from 1 to 2
- heights: int32 [8], replicated, may hold values from 8 to 16
- widths: int32 [8], replicated, may hold values from 64 to 128
- w_in: bfloat16 [3, 3, 3, 384, 16], replicated, may hold values from -0.3125 to 0.3125
- b_in: float32 [384], replicated, may hold values from -3 to 3
- gain_norm: float32 [384], replicated, may hold values from 0.5 to 1.5
- w_res: bfloat16 [3, 3, 3, 384, 384], replicated, may hold values from -0.0625 to 0.0625
- b_res: float32 [384], replicated, may hold values from -3 to 3
- w_time: bfloat16 [3, 768, 384], replicated, may hold values from -0.1875 to 0.1875
- b_time: float32 [768], replicated, may hold values from -3 to 3
- w_up: bfloat16 [3, 3, 192, 384], replicated, may hold values from -0.109375 to 0.109375
- b_up: float32 [192], replicated, may hold values from -3 to 3
Outputs:
- decoded: bfloat16 [8, 192, 4, 32, 256], P('req', None, None, 'tile')
The draws below stay inside these ranges and needn't reach their ends.
Inputs may be any that keep to these rules, and one draw needn't show every extreme that they name: piece_dest is a permutation of the decoder slots. Requests are packed one after another in a drawn order, each request's rows frame after frame and row after row, so the 8 rows of one device are consecutive rows of one request and no device sends more than 4 rows to one device.
All inputs are finite; a program needn't handle non-finite values.
Results may differ from the reference program's by a relative error of at most 0.0075.
Values may be sent and summed in bfloat16 or wider, within the bound.
A program may use at most 192 MiB of HBM per device.

```python
import jax
import jax.numpy as jnp
from jax import lax

C_LAT = 16
C_MID = 384
C_OUT = 192
LFRAMES = 2
LROWS = 4
LCOLS = 128
SLOTS = 8
PIECES = 256
GROUPS = 8
HL = 16
N_TILE = 4


def draw_piece_dest(key, part):
    packed_order = jax.random.permutation(key, GROUPS).astype(jnp.int32)
    positions = jnp.arange(PIECES, dtype=jnp.int32)
    request_slot = positions // (LFRAMES * HL)
    within = positions % (LFRAMES * HL)
    frame_id = within // HL
    row_id = within % HL
    group_id = packed_order[request_slot]
    tile_id = row_id // LROWS
    local_row = row_id % LROWS
    return ((group_id * N_TILE + tile_id) * SLOTS + frame_id * LROWS + local_row).astype(jnp.int32)


def touch_ends(drawn, rng, low, high):
    dims = drawn.shape
    place = [jax.random.randint(jax.random.fold_in(rng, axis), (), 0, dims[axis]) for axis in range(len(dims))]
    drawn = drawn.at[tuple(place)].set(low)
    longest = dims.index(max(dims))
    place[longest] = (place[longest] + 1) % dims[longest]
    return drawn.at[tuple(place)].set(high)


def levels(stream_key, extent, split, low, high):
    def one(axis_at, shards_of):
        draws = jax.random.uniform(jax.random.fold_in(jax.random.fold_in(stream_key, 6), axis_at), (shards_of,), jnp.float32, low / len(split), high / len(split))
        return jnp.repeat(jnp.exp(draws), extent[axis_at] // shards_of).reshape((-1,) + (1,) * (len(extent) - axis_at - 1))

    factor_of = one(*split[0])
    for cut in split[1:]:
        factor_of = factor_of * one(*cut)
    return factor_of


def gaussian(stream_key, shape, width, reach, pieces=(), kind=jnp.bfloat16):
    array = width * jax.random.normal(stream_key, shape, jnp.float32)
    if pieces:
        array = array * levels(stream_key, shape, pieces, -0.22, 0.18)
    return jnp.clip(array, -reach, reach).astype(kind)


def setup_inputs(seed: int = 0) -> dict:
    keys = jax.random.split(jax.random.key(seed), 15)
    return {
        "latents": gaussian(keys[0], (PIECES, C_LAT, LCOLS), 1.0, 6.0, ((0, 32),)),
        "piece_dest": draw_piece_dest(jax.random.fold_in(keys[14], 71), 0),
        "frames": touch_ends(jax.random.randint(keys[2], (GROUPS,), 1, LFRAMES + 1), jax.random.fold_in(keys[2], 1), 1, LFRAMES).astype(jnp.int32),
        "heights": touch_ends(jax.random.randint(keys[3], (GROUPS,), HL // 2, HL + 1), jax.random.fold_in(keys[3], 1), HL // 2, HL).astype(jnp.int32),
        "widths": touch_ends(jax.random.randint(keys[4], (GROUPS,), LCOLS // 2, LCOLS + 1), jax.random.fold_in(keys[4], 1), LCOLS // 2, LCOLS).astype(jnp.int32),
        "w_in": gaussian(keys[5], (3, 3, 3, C_MID, C_LAT), (27 * C_LAT) ** -0.5, 0.3125),
        "b_in": gaussian(keys[6], (C_MID,), 0.5, 3.0, (), jnp.float32),
        "gain_norm": jnp.clip(1.0 + 0.1 * jax.random.normal(keys[7], (C_MID,), jnp.float32), 0.5, 1.5),
        "w_res": gaussian(keys[8], (3, 3, 3, C_MID, C_MID), (27 * C_MID) ** -0.5, 0.0625),
        "b_res": gaussian(keys[9], (C_MID,), 0.5, 3.0, (), jnp.float32),
        "w_time": gaussian(keys[10], (3, 2 * C_MID, C_MID), (3 * C_MID) ** -0.5, 0.1875),
        "b_time": gaussian(keys[11], (2 * C_MID,), 0.5, 3.0, (), jnp.float32),
        "w_up": gaussian(keys[12], (3, 3, C_OUT, C_MID), (9 * C_MID) ** -0.5, 0.109375),
        "b_up": gaussian(keys[13], (C_OUT,), 0.5, 3.0, (), jnp.float32),
    }


def causal_conv(inputs, weight, offsets):
    frame_count, row_count, col_count = inputs.shape[1:]
    padded = jnp.pad(inputs, ((0, 0), (2, 0), (1, 1), (1, 1)))
    summed = jnp.zeros((weight.shape[3], frame_count, row_count, col_count), jnp.float32)
    for tap_t in range(3):
        for tap_r in range(3):
            for tap_c in range(3):
                summed = summed + jnp.einsum('oc,cthw->othw', weight[tap_t, tap_r, tap_c].astype(jnp.float32), padded[:, tap_t:tap_t + frame_count, tap_r:tap_r + row_count, tap_c:tap_c + col_count], precision=lax.Precision.HIGHEST)
    return summed + offsets[:, None, None, None]

def reference(latents, piece_dest, frames, heights, widths, w_in, b_in, gain_norm, w_res, b_res, w_time, b_time, w_up, b_up):
    arranged = jnp.zeros((PIECES, C_LAT, LCOLS), jnp.bfloat16).at[piece_dest].set(latents)
    latent_grid = arranged.reshape(GROUPS, N_TILE, LFRAMES, LROWS, C_LAT, LCOLS)
    latent_grid = latent_grid.transpose(0, 4, 2, 1, 3, 5).reshape(GROUPS, C_LAT, LFRAMES, HL, LCOLS)

    def decode_one(items):
        request_grid, frame_limit, row_limit, col_limit = items
        frame_ids = jnp.arange(LFRAMES, dtype=jnp.int32)
        row_ids = jnp.arange(HL, dtype=jnp.int32)
        col_ids = jnp.arange(LCOLS, dtype=jnp.int32)
        region = ((frame_ids < frame_limit)[:, None, None] & (row_ids < row_limit)[None, :, None] & (col_ids < col_limit)[None, None, :]).astype(jnp.float32)
        masked = (request_grid.astype(jnp.float32) * region).astype(jnp.bfloat16)
        first = causal_conv(masked.astype(jnp.float32), w_in, b_in).astype(jnp.bfloat16)
        first_f = first.astype(jnp.float32)
        scaled = first_f * lax.rsqrt(lax.optimization_barrier(jnp.mean(first_f * first_f, axis=0, keepdims=True)) + 1e-06) * gain_norm[:, None, None, None]
        normed = (jax.nn.silu(scaled) * region).astype(jnp.bfloat16)
        block = (first_f + causal_conv(normed.astype(jnp.float32), w_res, b_res)).astype(jnp.bfloat16)
        padded = jnp.pad(block.astype(jnp.float32), ((0, 0), (2, 0), (0, 0), (0, 0)))
        twice = jnp.zeros((2 * C_MID, LFRAMES, HL, LCOLS), jnp.float32)
        for tap_t in range(3):
            twice = twice + jnp.einsum('oc,cthw->othw', w_time[tap_t].astype(jnp.float32), padded[:, tap_t:tap_t + LFRAMES], precision=lax.Precision.HIGHEST)
        twice = twice + b_time[:, None, None, None]
        doubled = jnp.stack([twice[:C_MID], twice[C_MID:]], axis=2).reshape(C_MID, 2 * LFRAMES, HL, LCOLS)
        time_region = jnp.repeat(region, 2, axis=0)
        timed = (doubled * time_region).astype(jnp.bfloat16)
        widened = jnp.repeat(jnp.repeat(timed.astype(jnp.float32), 2, axis=2), 2, axis=3)
        padded_up = jnp.pad(widened, ((0, 0), (0, 0), (1, 1), (1, 1)))
        summed = jnp.zeros((C_OUT, 2 * LFRAMES, 2 * HL, 2 * LCOLS), jnp.float32)
        for tap_r in range(3):
            for tap_c in range(3):
                summed = summed + jnp.einsum('oc,cthw->othw', w_up[tap_r, tap_c].astype(jnp.float32), padded_up[:, :, tap_r:tap_r + 2 * HL, tap_c:tap_c + 2 * LCOLS], precision=lax.Precision.HIGHEST)
        summed = summed + b_up[:, None, None, None]
        out_region = jnp.repeat(jnp.repeat(time_region, 2, axis=1), 2, axis=2)
        return (summed * out_region).astype(jnp.bfloat16)
    return lax.map(decode_one, (latent_grid, frames, heights, widths))
```

```python
import functools

import jax
import jax.numpy as jnp
from jax import lax
from jax.experimental import pallas as pl
from jax.experimental.pallas import tpu as pltpu
from jax.sharding import PartitionSpec as P

LFRAMES = 2
MESH = pl.DeviceIdType.MESH
F32 = jnp.float32
BF16 = jnp.bfloat16


def route_kernel(
    n_req, n_tile, dest_ref, lat_ref, out_ref, buf, sel, send_sem, recv_sem, side_send, side_recv
):
    g = lax.axis_index("req")
    t = lax.axis_index("tile")
    half = n_tile // 2
    slots = lat_ref.shape[0]
    rows = slots // LFRAMES

    barrier = pltpu.get_barrier_semaphore()

    def greet(k, carry):
        other = lax.rem(g + k, n_req)
        for f in range(LFRAMES):
            source = f * half + t // 2

            @pl.when((k > 0) | (source != t))
            def _():
                pl.semaphore_signal(
                    barrier, inc=1, device_id=(other, source), device_id_type=MESH
                )

        return carry

    lax.fori_loop(0, n_req, greet, 0)

    @pl.when(t > 0)
    def _():
        pl.semaphore_signal(barrier, inc=1, device_id=(g, t - 1), device_id_type=MESH)

    @pl.when(t < n_tile - 1)
    def _():
        pl.semaphore_signal(barrier, inc=1, device_id=(g, t + 1), device_id_type=MESH)

    inner = (t + n_tile - 1) // n_tile - (t + 1) // n_tile
    pl.semaphore_wait(barrier, 2 * n_req + 2 * inner)

    frame = t // half
    first_tile = 2 * lax.rem(t, half)

    def remote(k, h):
        return pltpu.make_async_remote_copy(
            src_ref=lat_ref.at[pl.ds(h * rows, rows)],
            dst_ref=buf.at[g, frame],
            send_sem=send_sem.at[k, h],
            recv_sem=recv_sem.at[g, frame],
            device_id=(lax.rem(g + k, n_req), first_tile + h),
            device_id_type=MESH,
        )

    def local(h):
        return pltpu.make_async_copy(
            lat_ref.at[pl.ds(h * rows, rows)], buf.at[g, frame], recv_sem.at[g, frame]
        )

    def send(k, carry):
        for h in range(2):

            @pl.when((k > 0) | (first_tile + h != t))
            def _():
                remote(k, h).start()

            @pl.when((k == 0) & (first_tile + h == t))
            def _():
                local(h).start()

        return carry

    lax.fori_loop(0, n_req, send, 0)

    def arrive(s, carry):
        for f in range(LFRAMES):
            pltpu.make_async_copy(buf.at[s, f], buf.at[s, f], recv_sem.at[s, f]).wait()
        return carry

    lax.fori_loop(0, n_req, arrive, 0)

    per = slots * n_tile
    source = jnp.int32(0)
    for j in range(n_req):
        source = jnp.where(dest_ref[j * per] // per == g, j, source)
    sel[:, 3 : 3 + rows] = buf[source]

    up = pltpu.make_async_remote_copy(
        src_ref=sel.at[:, pl.ds(3, 3)],
        dst_ref=sel.at[:, pl.ds(3 + rows, 3)],
        send_sem=side_send.at[0],
        recv_sem=side_recv.at[0],
        device_id=(g, t - 1),
        device_id_type=MESH,
    )
    down = pltpu.make_async_remote_copy(
        src_ref=sel.at[:, pl.ds(rows, 3)],
        dst_ref=sel.at[:, pl.ds(0, 3)],
        send_sem=side_send.at[1],
        recv_sem=side_recv.at[1],
        device_id=(g, t + 1),
        device_id_type=MESH,
    )
    zeros = jnp.zeros((LFRAMES, 3) + lat_ref.shape[1:], BF16)

    @pl.when(t > 0)
    def _():
        up.start()

    @pl.when(t < n_tile - 1)
    def _():
        down.start()

    @pl.when(t == 0)
    def _():
        sel[:, 0:3] = zeros

    @pl.when(t == n_tile - 1)
    def _():
        sel[:, 3 + rows :] = zeros

    def sent(k, carry):
        for h in range(2):

            @pl.when((k > 0) | (first_tile + h != t))
            def _():
                remote(k, h).wait_send()

        return carry

    lax.fori_loop(0, n_req, sent, 0)

    @pl.when(t > 0)
    def _():
        up.wait_send()
        down.wait_recv()

    @pl.when(t < n_tile - 1)
    def _():
        down.wait_send()
        up.wait_recv()

    out_ref[...] = sel[...]


def route(n_req, n_tile, piece_dest, latents):
    slots, channels, cols = latents.shape
    rows = slots // LFRAMES
    return pl.pallas_call(
        functools.partial(route_kernel, n_req, n_tile),
        out_shape=jax.ShapeDtypeStruct((LFRAMES, rows + 6, channels, cols), BF16),
        in_specs=[
            pl.BlockSpec(memory_space=pltpu.SMEM),
            pl.BlockSpec(memory_space=pltpu.VMEM),
        ],
        out_specs=pl.BlockSpec(memory_space=pltpu.VMEM),
        scratch_shapes=[
            pltpu.VMEM((n_req, LFRAMES, rows, channels, cols), BF16),
            pltpu.VMEM((LFRAMES, rows + 6, channels, cols), BF16),
            pltpu.SemaphoreType.DMA((n_req, 2)),
            pltpu.SemaphoreType.DMA((n_req, LFRAMES)),
            pltpu.SemaphoreType.DMA((2,)),
            pltpu.SemaphoreType.DMA((2,)),
        ],
        compiler_params=pltpu.CompilerParams(
            collective_id=0, has_side_effects=True, vmem_limit_bytes=16 * 2**20
        ),
        name="route",
    )(piece_dest, latents)


def shift(x, by):
    width = x.shape[1]
    lane = lax.broadcasted_iota(jnp.int32, x.shape, 1)
    if by == 1:
        return jnp.where(lane == 0, 0.0, pltpu.roll(x, 1, axis=1))
    return jnp.where(lane == width - 1, 0.0, pltpu.roll(x, width - 1, axis=1))


def column(ref):
    n = ref.shape[1]
    return jnp.transpose(jnp.broadcast_to(ref[...], (128, n)))


def decode_kernel(
    frames_ref,
    heights_ref,
    widths_ref,
    grid_ref,
    w_in_ref,
    b_in_ref,
    gain_ref,
    b_res_ref,
    b_time_ref,
    b_up_ref,
    w_res_hbm,
    w_time_hbm,
    w_up_hbm,
    out_ref,
    w_in,
    wr,
    wt,
    wu_raw,
    wu,
    x_in,
    first,
    spread,
    timed,
    inter,
    perm,
    c_in,
    c_gain,
    c_res,
    c_time,
    c_up,
    sem_r,
    sem_t,
    sem_u,
):
    g = lax.axis_index("req")
    t = lax.axis_index("tile")
    channels, cols = grid_ref.shape[2], grid_ref.shape[3]
    rows = grid_ref.shape[1] - 6
    mid = w_in_ref.shape[1]
    outc = b_up_ref.shape[1]
    one = 9 * channels
    mrows = rows + 4

    copies_r = []
    for d in range(3):
        for a in range(2):
            for e in range(3):
                at = (a * 3 + e) * mid
                copies_r.append(
                    pltpu.make_async_copy(
                        w_res_hbm.at[a + 1, d, e],
                        wr.at[d, :, pl.ds(at, mid)],
                        sem_r.at[d, a * 3 + e],
                    )
                )
    copies_t = [
        pltpu.make_async_copy(w_time_hbm.at[a + 1], wt.at[:, pl.ds(a * mid, mid)], sem_t.at[a])
        for a in range(2)
    ]
    copy_u = pltpu.make_async_copy(w_up_hbm, wu_raw, sem_u)
    for copy in copies_r + copies_t:
        copy.start()
    copy_u.start()

    taps = jnp.concatenate([w_in_ref[2 * one :], w_in_ref[one : 2 * one]], axis=0)
    w_in[...] = jnp.transpose(taps)
    c_in[...] = column(b_in_ref)
    c_gain[...] = column(gain_ref)
    c_res[...] = column(b_res_ref)
    c_time[...] = column(b_time_ref)
    c_up[...] = column(b_up_ref)
    src = lax.broadcasted_iota(jnp.int32, (2 * cols, 2 * cols), 0)
    dst = lax.broadcasted_iota(jnp.int32, (2 * cols, 2 * cols), 1)
    perm[...] = jnp.where(
        (src % cols == dst // 2) & (src // cols == dst % 2), 1.0, 0.0
    ).astype(BF16)

    n_frames, n_rows, n_cols = frames_ref[g], heights_ref[g], widths_ref[g]
    lane = lax.broadcasted_iota(jnp.int32, (1, cols), 1)

    def mask(f, r):
        live = (f < n_frames) & (r >= 0) & (r < n_rows)
        return lane < jnp.where(live, n_cols, 0)

    def mask2(f, r):
        return jnp.concatenate([mask(f, r), mask(f, r + 1)], axis=1)

    def wide(ref):
        return jnp.concatenate([ref[...], ref[...]], axis=1)

    for f in range(LFRAMES):
        base = (1 - f) * one
        for q in range(rows + 6):
            x = grid_ref[f, q].astype(F32)
            x = jnp.where(mask(f, rows * t - 3 + q), x, 0.0)
            for e, y in enumerate((shift(x, 1), x, shift(x, -1))):
                y = y.astype(BF16)
                for d in range(3):
                    if 0 <= q - d < mrows:
                        at = base + (d * 3 + e) * channels
                        x_in[at : at + channels, (q - d) * cols : (q - d + 1) * cols] = y

    def stage_first(p, carry):
        at = pl.multiple_of(p * 2 * cols, 2 * cols)
        for f in range(LFRAMES):
            if f == 0:
                acc = jnp.dot(
                    w_in[:, 0:one],
                    x_in[one : 2 * one, pl.ds(at, 2 * cols)],
                    preferred_element_type=F32,
                )
            else:
                acc = jnp.dot(
                    w_in[...], x_in[:, pl.ds(at, 2 * cols)], preferred_element_type=F32
                )
            half = (acc + wide(c_in)).astype(BF16)
            first[f, :, pl.ds(at, 2 * cols)] = half
            v = half.astype(F32)
            mean = jnp.sum(v * v, axis=0, keepdims=True) * (1.0 / mid)
            v = v * lax.rsqrt(mean + 1e-06) * wide(c_gain)
            v = v / (1.0 + jnp.exp(-v))
            v = jnp.where(mask2(f, rows * t - 2 + 2 * p), v, 0.0)
            for e in range(3):
                parts = [v[:, i * cols : (i + 1) * cols] for i in range(2)]
                if e != 1:
                    parts = [shift(part, 1 - e) for part in parts]
                spread[
                    (f * 3 + e) * mid : (f * 3 + e + 1) * mid, pl.ds(at, 2 * cols)
                ] = jnp.concatenate(parts, axis=1).astype(BF16)
        return carry

    lax.fori_loop(0, mrows // 2, stage_first, 0)

    for copy in copies_r:
        copy.wait()
    for copy in copies_t:
        copy.wait()

    def stage_block(p, carry):
        at = pl.multiple_of(p * 2 * cols, 2 * cols)
        here = pl.ds(pl.multiple_of(at + cols, cols), 2 * cols)
        accs = [first[f, :, here].astype(F32) + wide(c_res) for f in range(LFRAMES)]
        for d in range(3):
            there = pl.ds(pl.multiple_of(at + d * cols, cols), 2 * cols)
            accs[0] = accs[0] + jnp.dot(
                wr[d, :, 3 * mid :], spread[0 : 3 * mid, there], preferred_element_type=F32
            )
            accs[1] = accs[1] + jnp.dot(
                wr[d], spread[:, there], preferred_element_type=F32
            )
        blocks = [acc.astype(BF16) for acc in accs]
        both = jnp.concatenate(blocks, axis=0)
        for f in range(LFRAMES):
            if f == 0:
                twice = jnp.dot(wt[:, mid:], blocks[0], preferred_element_type=F32)
            else:
                twice = jnp.dot(wt[...], both, preferred_element_type=F32)
            twice = jnp.where(mask2(f, rows * t - 1 + 2 * p), twice + wide(c_time), 0.0)
            twice = twice.astype(BF16)
            for k in range(2):
                timed[2 * f + k, :, pl.ds(at, 2 * cols)] = twice[k * mid : (k + 1) * mid]
        return carry

    lax.fori_loop(0, (rows + 2) // 2, stage_block, 0)

    copy_u.wait()
    w0, w1, w2 = [wu_raw[d].reshape(3 * outc, mid) for d in range(3)]
    wu[0, :, 0:mid] = w0
    wu[0, :, mid:] = (w1.astype(F32) + w2.astype(F32)).astype(BF16)
    wu[1, :, 0:mid] = (w0.astype(F32) + w1.astype(F32)).astype(BF16)
    wu[1, :, mid:] = w2

    def stage_up(f, carry):
        for p in range(rows // 2):
            x = [timed[f, :, (2 * p + i) * cols : (2 * p + i + 2) * cols] for i in range(3)]
            for k in range(2):
                z = jnp.dot(
                    wu[k],
                    jnp.concatenate([x[k], x[k + 1]], axis=0),
                    preferred_element_type=F32,
                )
                for i in range(2):
                    r = 2 * p + i
                    z0, z1, z2 = [
                        z[e * outc : (e + 1) * outc, i * cols : (i + 1) * cols] for e in range(3)
                    ]
                    live = mask(f // 2, rows * t + r)
                    base = z1 + c_up[...]
                    even = jnp.where(live, shift(z0, 1) + z2 + base, 0.0)
                    odd = jnp.where(live, z0 + shift(z2, -1) + base, 0.0)
                    pair = jnp.concatenate([even, odd], axis=1).astype(BF16)
                    row = jnp.dot(pair, perm[...], preferred_element_type=F32)
                    for w in range(2):
                        inter[w, pl.ds(2 * r + k, outc, stride=2 * rows), :] = row[
                            :, w * cols : (w + 1) * cols
                        ]
        for w in range(2):
            out_ref[0, :, f, :, w * cols : (w + 1) * cols] = (
                inter[w].reshape(outc, 2 * rows, cols).astype(BF16)
            )
        return carry

    lax.fori_loop(0, 2 * LFRAMES, stage_up, 0)


def decode(grid, frames, heights, widths, w_in, biases, w_res, w_time, w_up):
    rows, cols = grid.shape[1] - 6, grid.shape[3]
    channels = grid.shape[2]
    mid, outc = w_res.shape[3], w_up.shape[2]
    smem = pl.BlockSpec(memory_space=pltpu.SMEM)
    vmem = pl.BlockSpec(memory_space=pltpu.VMEM)
    anywhere = pl.BlockSpec(memory_space=pl.ANY)
    return pl.pallas_call(
        decode_kernel,
        out_shape=jax.ShapeDtypeStruct((1, outc, 2 * LFRAMES, 2 * rows, 2 * cols), BF16),
        in_specs=[smem] * 3 + [vmem] * 7 + [anywhere] * 3,
        out_specs=vmem,
        scratch_shapes=[
            pltpu.VMEM((mid, 18 * channels), BF16),
            pltpu.VMEM((3, mid, 6 * mid), BF16),
            pltpu.VMEM((2 * mid, 2 * mid), BF16),
            pltpu.VMEM(w_up.shape, BF16),
            pltpu.VMEM((2, 3 * outc, 2 * mid), BF16),
            pltpu.VMEM((18 * channels, (rows + 4) * cols), BF16),
            pltpu.VMEM((LFRAMES, mid, (rows + 4) * cols), BF16),
            pltpu.VMEM((6 * mid, (rows + 4) * cols), BF16),
            pltpu.VMEM((2 * LFRAMES, mid, (rows + 2) * cols), BF16),
            pltpu.VMEM((2, outc * 2 * rows, cols), F32),
            pltpu.VMEM((2 * cols, 2 * cols), BF16),
            pltpu.VMEM((mid, 128), F32),
            pltpu.VMEM((mid, 128), F32),
            pltpu.VMEM((mid, 128), F32),
            pltpu.VMEM((2 * mid, 128), F32),
            pltpu.VMEM((outc, 128), F32),
            pltpu.SemaphoreType.DMA((3, 6)),
            pltpu.SemaphoreType.DMA((2,)),
            pltpu.SemaphoreType.DMA,
        ],
        compiler_params=pltpu.CompilerParams(vmem_limit_bytes=48 * 2**20),
        name="decode",
    )(frames, heights, widths, grid, w_in, *biases, w_res, w_time, w_up)


def solution(mesh):
    n_req, n_tile = mesh.shape["req"], mesh.shape["tile"]

    def on_device(
        latents, piece_dest, frames, heights, widths,
        w_in, b_in, gain_norm, w_res, b_res, w_time, b_time, w_up, b_up,
    ):
        grid = route(n_req, n_tile, piece_dest, latents)
        mid, channels = w_in.shape[3], w_in.shape[4]
        taps = jnp.transpose(w_in, (0, 1, 2, 4, 3)).reshape(27 * channels, mid)
        biases = [b.reshape(1, -1) for b in (b_in, gain_norm, b_res, b_time, b_up)]
        return decode(grid, frames, heights, widths, taps, biases, w_res, w_time, w_up)

    return jax.shard_map(
        on_device,
        mesh=mesh,
        in_specs=(P(("req", "tile"), None, None),) + (P(),) * 13,
        out_specs=P("req", None, None, "tile", None),
        check_vma=False,
    )
```

```python
import functools

import jax
import jax.numpy as jnp
from jax import lax
from jax.experimental import pallas as pl
from jax.experimental.pallas import tpu as pltpu
from jax.sharding import PartitionSpec as P

LFRAMES = 2
MESH = pl.DeviceIdType.MESH
VMEM_BYTES = 63 * 2**20
F32 = jnp.float32
BF16 = jnp.bfloat16


def route_kernel(
    n_req, n_tile, dest_hbm, lat_ref, out_ref,
    dest_ref, buf, sel, dest_sem, send_sem, recv_sem, side_send, side_recv,
):
    g = lax.axis_index("req")
    t = lax.axis_index("tile")
    half = n_tile // 2
    slots = lat_ref.shape[0]
    rows = slots // LFRAMES

    fetch = pltpu.make_async_copy(dest_hbm, dest_ref, dest_sem)
    fetch.start()
    barrier = pltpu.get_barrier_semaphore()

    def greet(k, carry):
        other = lax.rem(g + k, n_req)
        for f in range(LFRAMES):
            source = f * half + t // 2

            @pl.when((k > 0) | (source != t))
            def _():
                pl.semaphore_signal(
                    barrier, inc=1, device_id=(other, source), device_id_type=MESH
                )

        return carry

    lax.fori_loop(0, n_req, greet, 0)

    @pl.when(t > 0)
    def _():
        pl.semaphore_signal(barrier, inc=1, device_id=(g, t - 1), device_id_type=MESH)

    @pl.when(t < n_tile - 1)
    def _():
        pl.semaphore_signal(barrier, inc=1, device_id=(g, t + 1), device_id_type=MESH)

    inner = (t + n_tile - 1) // n_tile - (t + 1) // n_tile
    pl.semaphore_wait(barrier, 2 * n_req + 2 * inner)

    frame = t // half
    first_tile = 2 * lax.rem(t, half)

    def remote(k, h):
        return pltpu.make_async_remote_copy(
            src_ref=lat_ref.at[pl.ds(h * rows, rows)],
            dst_ref=buf.at[g, frame],
            send_sem=send_sem.at[k, h],
            recv_sem=recv_sem.at[g, frame],
            device_id=(lax.rem(g + k, n_req), first_tile + h),
            device_id_type=MESH,
        )

    def local(h):
        return pltpu.make_async_copy(
            lat_ref.at[pl.ds(h * rows, rows)], buf.at[g, frame], recv_sem.at[g, frame]
        )

    def send(k, carry):
        for h in range(2):

            @pl.when((k > 0) | (first_tile + h != t))
            def _():
                remote(k, h).start()

            @pl.when((k == 0) & (first_tile + h == t))
            def _():
                local(h).start()

        return carry

    lax.fori_loop(0, n_req, send, 0)

    def arrive(s, carry):
        for f in range(LFRAMES):
            pltpu.make_async_copy(buf.at[s, f], buf.at[s, f], recv_sem.at[s, f]).wait()
        return carry

    lax.fori_loop(0, n_req, arrive, 0)

    fetch.wait()
    per = slots * n_tile
    source = jnp.int32(0)
    for j in range(n_req):
        source = jnp.where(dest_ref[j * per] // per == g, j, source)
    sel[:, 3 : 3 + rows] = buf[source]

    up = pltpu.make_async_remote_copy(
        src_ref=sel.at[:, pl.ds(3, 3)],
        dst_ref=sel.at[:, pl.ds(3 + rows, 3)],
        send_sem=side_send.at[0],
        recv_sem=side_recv.at[0],
        device_id=(g, t - 1),
        device_id_type=MESH,
    )
    down = pltpu.make_async_remote_copy(
        src_ref=sel.at[:, pl.ds(rows, 3)],
        dst_ref=sel.at[:, pl.ds(0, 3)],
        send_sem=side_send.at[1],
        recv_sem=side_recv.at[1],
        device_id=(g, t + 1),
        device_id_type=MESH,
    )
    zeros = jnp.zeros((LFRAMES, 3) + lat_ref.shape[1:], BF16)

    @pl.when(t > 0)
    def _():
        up.start()

    @pl.when(t < n_tile - 1)
    def _():
        down.start()

    @pl.when(t == 0)
    def _():
        sel[:, 0:3] = zeros

    @pl.when(t == n_tile - 1)
    def _():
        sel[:, 3 + rows :] = zeros

    def sent(k, carry):
        for h in range(2):

            @pl.when((k > 0) | (first_tile + h != t))
            def _():
                remote(k, h).wait_send()

        return carry

    lax.fori_loop(0, n_req, sent, 0)

    @pl.when(t > 0)
    def _():
        up.wait_send()
        down.wait_recv()

    @pl.when(t < n_tile - 1)
    def _():
        down.wait_send()
        up.wait_recv()

    out_ref[...] = sel[...]


def route(n_req, n_tile, piece_dest, latents):
    slots, channels, cols = latents.shape
    rows = slots // LFRAMES
    return pl.pallas_call(
        functools.partial(route_kernel, n_req, n_tile),
        out_shape=jax.ShapeDtypeStruct((LFRAMES, rows + 6, channels, cols), BF16),
        in_specs=[pl.BlockSpec(memory_space=pltpu.HBM)] * 2,
        out_specs=pl.BlockSpec(memory_space=pltpu.VMEM),
        scratch_shapes=[
            pltpu.SMEM(piece_dest.shape, jnp.int32),
            pltpu.VMEM((n_req, LFRAMES, rows, channels, cols), BF16),
            pltpu.VMEM((LFRAMES, rows + 6, channels, cols), BF16),
            pltpu.SemaphoreType.DMA,
            pltpu.SemaphoreType.DMA((n_req, 2)),
            pltpu.SemaphoreType.DMA((n_req, LFRAMES)),
            pltpu.SemaphoreType.DMA((2,)),
            pltpu.SemaphoreType.DMA((2,)),
        ],
        compiler_params=pltpu.CompilerParams(
            collective_id=0, has_side_effects=True, vmem_limit_bytes=VMEM_BYTES
        ),
        name="route",
    )(piece_dest, latents)


def shift(x, by):
    width = x.shape[1]
    lane = lax.broadcasted_iota(jnp.int32, x.shape, 1)
    if by == 1:
        return jnp.where(lane == 0, 0.0, pltpu.roll(x, 1, axis=1))
    return jnp.where(lane == width - 1, 0.0, pltpu.roll(x, width - 1, axis=1))


def column(ref):
    n = ref.shape[0]
    return jnp.transpose(jnp.broadcast_to(ref[...].reshape(1, n), (128, n)))


def decode_kernel(grid_ref, *refs):
    hbm, (out_ref, *refs) = refs[:12], refs[12:]
    frames_hbm, heights_hbm, widths_hbm, w_in_hbm = hbm[:4]
    vector_hbm, (w_res_hbm, w_time_hbm, w_up_hbm) = hbm[4:9], hbm[9:]
    frames_ref, heights_ref, widths_ref, *refs = refs
    vectors, refs = refs[:5], refs[5:]
    taps, w_in, wr, wt, wu_raw, wu, x_in, first, spread, timed, inter, perm, *refs = refs
    c_in, c_gain, c_res, c_time, c_up, sem_s, sem_v, sem_i, sem_r, sem_t, sem_u = refs
    g = lax.axis_index("req")
    t = lax.axis_index("tile")
    channels, cols = grid_ref.shape[2], grid_ref.shape[3]
    rows = grid_ref.shape[1] - 6
    mid = taps.shape[1]
    outc = wu_raw.shape[2]
    one = 9 * channels
    mrows = rows + 4

    copies_s = [
        pltpu.make_async_copy(a, b, sem_s.at[i])
        for i, (a, b) in enumerate(
            zip((frames_hbm, heights_hbm, widths_hbm), (frames_ref, heights_ref, widths_ref))
        )
    ]
    copies_v = [
        pltpu.make_async_copy(a, b, sem_v.at[i])
        for i, (a, b) in enumerate(zip(vector_hbm, vectors))
    ]
    copies_i = [
        pltpu.make_async_copy(
            w_in_hbm.at[pl.ds((2 - i) * one, one)], taps.at[pl.ds(i * one, one)], sem_i.at[i]
        )
        for i in range(2)
    ]
    copies_r = []
    for d in range(3):
        for a in range(2):
            for e in range(3):
                copies_r.append(
                    pltpu.make_async_copy(
                        w_res_hbm.at[2 - a, d, e],
                        wr.at[pl.ds(a * mid, mid), pl.ds((d * 3 + e) * mid, mid)],
                        sem_r.at[d, a * 3 + e],
                    )
                )
    copies_t = [
        pltpu.make_async_copy(w_time_hbm.at[a + 1], wt.at[:, pl.ds(a * mid, mid)], sem_t.at[a])
        for a in range(2)
    ]
    copy_u = pltpu.make_async_copy(w_up_hbm, wu_raw, sem_u)
    for copy in copies_s + copies_v + copies_i + copies_r + copies_t + [copy_u]:
        copy.start()

    for copy in copies_s + copies_v + copies_i:
        copy.wait()
    w_in[...] = jnp.transpose(taps[...])
    for kept, vector in zip((c_in, c_gain, c_res, c_time, c_up), vectors):
        kept[...] = column(vector)
    src = lax.broadcasted_iota(jnp.int32, (2 * cols, 2 * cols), 0)
    dst = lax.broadcasted_iota(jnp.int32, (2 * cols, 2 * cols), 1)
    perm[...] = jnp.where(
        (src % cols == dst // 2) & (src // cols == dst % 2), 1.0, 0.0
    ).astype(BF16)

    n_frames, n_rows, n_cols = frames_ref[g], heights_ref[g], widths_ref[g]
    lane = lax.broadcasted_iota(jnp.int32, (1, cols), 1)

    def mask(f, r):
        live = (f < n_frames) & (r >= 0) & (r < n_rows)
        return lane < jnp.where(live, n_cols, 0)

    def masks(f, r, n):
        return jnp.concatenate([mask(f, r + i) for i in range(n)], axis=1)

    def wide(ref, n):
        return jnp.concatenate([ref[...]] * n, axis=1)

    for f in range(LFRAMES):
        base = (1 - f) * one
        for q in range(rows + 6):
            x = grid_ref[f, q].astype(F32)
            x = jnp.where(mask(f, rows * t - 3 + q), x, 0.0)
            for e, y in enumerate((shift(x, 1), x, shift(x, -1))):
                y = y.astype(BF16)
                for d in range(3):
                    if 0 <= q - d < mrows:
                        at = base + (d * 3 + e) * channels
                        x_in[at : at + channels, (q - d) * cols : (q - d + 1) * cols] = y

    span = mrows // 2

    def stage_first(p, carry):
        at = pl.multiple_of(p * span * cols, span * cols)
        here = pl.ds(at, span * cols)
        for f in range(LFRAMES):
            if f == 0:
                x = x_in[one : 2 * one, here]
            else:
                x = x_in[:, here]
            acc = jnp.dot(w_in[:, 0 : x.shape[0]], x, preferred_element_type=F32)
            half = (acc + wide(c_in, span)).astype(BF16)
            first[f, :, here] = half
            v = half.astype(F32)
            mean = jnp.sum(v * v, axis=0, keepdims=True) * (1.0 / mid)
            v = v * lax.rsqrt(mean + 1e-06) * wide(c_gain, span)
            v = v / (1.0 + jnp.exp(-v))
            v = jnp.where(masks(f, rows * t - 2 + span * p, span), v, 0.0)
            parts = [v[:, i * cols : (i + 1) * cols] for i in range(span)]
            for e in range(3):
                moved = parts if e == 1 else [shift(part, 1 - e) for part in parts]
                spread[(f * 3 + e) * mid : (f * 3 + e + 1) * mid, here] = jnp.concatenate(
                    moved, axis=1
                ).astype(BF16)
        return carry

    lax.fori_loop(0, 2, stage_first, 0)

    for copy in copies_r + copies_t:
        copy.wait()

    brows = rows + 2
    taller = [
        jnp.concatenate(
            [
                spread[f * 3 * mid : (f + 1) * 3 * mid, d * cols : (d + brows) * cols]
                for d in range(3)
            ],
            axis=0,
        )
        for f in range(LFRAMES)
    ]
    old = jnp.dot(wr[...], taller[0], preferred_element_type=F32)
    new = jnp.dot(wr[0:mid], taller[1], preferred_element_type=F32)
    blocks = []
    for f, acc in enumerate((old[0:mid], old[mid:] + new)):
        kept = first[f, :, cols : (brows + 1) * cols].astype(F32)
        blocks.append((acc + wide(c_res, brows) + kept).astype(BF16))
    for f in range(LFRAMES):
        if f == 0:
            twice = jnp.dot(wt[:, mid:], blocks[0], preferred_element_type=F32)
        else:
            both = jnp.concatenate(blocks, axis=0)
            twice = jnp.dot(wt[...], both, preferred_element_type=F32)
        live = masks(f, rows * t - 1, brows)
        twice = jnp.where(live, twice + wide(c_time, brows), 0.0).astype(BF16)
        for k in range(2):
            timed[2 * f + k] = twice[k * mid : (k + 1) * mid]

    copy_u.wait()
    w0, w1, w2 = [wu_raw[d].reshape(3 * outc, mid) for d in range(3)]
    wu[0, :, 0:mid] = w0
    wu[0, :, mid:] = (w1.astype(F32) + w2.astype(F32)).astype(BF16)
    wu[1, :, 0:mid] = (w0.astype(F32) + w1.astype(F32)).astype(BF16)
    wu[1, :, mid:] = w2

    def stage_up(f, carry):
        x = [timed[f, :, i * cols : (i + rows) * cols] for i in range(3)]
        for k in range(2):
            z = jnp.dot(
                wu[k],
                jnp.concatenate([x[k], x[k + 1]], axis=0),
                preferred_element_type=F32,
            )
            for r in range(rows):
                z0, z1, z2 = [
                    z[e * outc : (e + 1) * outc, r * cols : (r + 1) * cols] for e in range(3)
                ]
                live = mask(f // 2, rows * t + r)
                base = z1 + c_up[...]
                even = jnp.where(live, shift(z0, 1) + z2 + base, 0.0)
                odd = jnp.where(live, z0 + shift(z2, -1) + base, 0.0)
                pair = jnp.concatenate([even, odd], axis=1).astype(BF16)
                row = jnp.dot(pair, perm[...], preferred_element_type=F32)
                for w in range(2):
                    inter[w, pl.ds(2 * r + k, outc, stride=2 * rows), :] = row[
                        :, w * cols : (w + 1) * cols
                    ]
        for w in range(2):
            out_ref[0, :, f, :, w * cols : (w + 1) * cols] = (
                inter[w].reshape(outc, 2 * rows, cols).astype(BF16)
            )
        return carry

    lax.fori_loop(0, 2 * LFRAMES, stage_up, 0)


def decode(grid, frames, heights, widths, w_in, vectors, w_res, w_time, w_up):
    rows, cols = grid.shape[1] - 6, grid.shape[3]
    channels = grid.shape[2]
    mid, outc = w_res.shape[3], w_up.shape[2]
    vmem = pl.BlockSpec(memory_space=pltpu.VMEM)
    return pl.pallas_call(
        decode_kernel,
        out_shape=jax.ShapeDtypeStruct((1, outc, 2 * LFRAMES, 2 * rows, 2 * cols), BF16),
        in_specs=[vmem] + [pl.BlockSpec(memory_space=pltpu.HBM)] * 12,
        out_specs=vmem,
        scratch_shapes=[pltpu.SMEM(v.shape, jnp.int32) for v in (frames, heights, widths)]
        + [pltpu.VMEM(v.shape, F32) for v in vectors]
        + [
            pltpu.VMEM((18 * channels, mid), BF16),
            pltpu.VMEM((mid, 18 * channels), BF16),
            pltpu.VMEM((2 * mid, 9 * mid), BF16),
            pltpu.VMEM((2 * mid, 2 * mid), BF16),
            pltpu.VMEM(w_up.shape, BF16),
            pltpu.VMEM((2, 3 * outc, 2 * mid), BF16),
            pltpu.VMEM((18 * channels, (rows + 4) * cols), BF16),
            pltpu.VMEM((LFRAMES, mid, (rows + 4) * cols), BF16),
            pltpu.VMEM((6 * mid, (rows + 4) * cols), BF16),
            pltpu.VMEM((2 * LFRAMES, mid, (rows + 2) * cols), BF16),
            pltpu.VMEM((2, outc * 2 * rows, cols), F32),
            pltpu.VMEM((2 * cols, 2 * cols), BF16),
            pltpu.VMEM((mid, 128), F32),
            pltpu.VMEM((mid, 128), F32),
            pltpu.VMEM((mid, 128), F32),
            pltpu.VMEM((2 * mid, 128), F32),
            pltpu.VMEM((outc, 128), F32),
            pltpu.SemaphoreType.DMA((3,)),
            pltpu.SemaphoreType.DMA((5,)),
            pltpu.SemaphoreType.DMA((2,)),
            pltpu.SemaphoreType.DMA((3, 6)),
            pltpu.SemaphoreType.DMA((2,)),
            pltpu.SemaphoreType.DMA,
        ],
        compiler_params=pltpu.CompilerParams(vmem_limit_bytes=VMEM_BYTES),
        name="decode",
    )(grid, frames, heights, widths, w_in, *vectors, w_res, w_time, w_up)


def solution(mesh):
    n_req, n_tile = mesh.shape["req"], mesh.shape["tile"]

    def on_device(
        latents, piece_dest, frames, heights, widths,
        w_in, b_in, gain_norm, w_res, b_res, w_time, b_time, w_up, b_up,
    ):
        grid = route(n_req, n_tile, piece_dest, latents)
        mid, channels = w_in.shape[3], w_in.shape[4]
        taps = jnp.transpose(w_in, (0, 1, 2, 4, 3)).reshape(27 * channels, mid)
        vectors = (b_in, gain_norm, b_res, b_time, b_up)
        return decode(grid, frames, heights, widths, taps, vectors, w_res, w_time, w_up)

    return jax.shard_map(
        on_device,
        mesh=mesh,
        in_specs=(P(("req", "tile"), None, None),) + (P(),) * 13,
        out_specs=P("req", None, None, "tile", None),
        check_vma=False,
    )
```

```python
import functools

import jax
import jax.numpy as jnp
from jax import lax
from jax.experimental import pallas as pl
from jax.experimental.pallas import tpu as pltpu
from jax.sharding import PartitionSpec as P

LFRAMES = 2
MESH = pl.DeviceIdType.MESH
VMEM_BYTES = 63 * 2**20
F32 = jnp.float32
BF16 = jnp.bfloat16


def route_kernel(
    n_req, n_tile, dest_hbm, lat_ref, out_ref,
    dest_ref, held, item, land, dest_sem, send_sem, recv_sem, send_two, recv_two,
):
    g = lax.axis_index("req")
    t = lax.axis_index("tile")
    far = n_req // 2 if n_req < 8 else 4
    low = n_req // far
    line, place = g // low, lax.rem(g, low)
    half = n_tile // 2
    slots = lat_ref.shape[0]
    rows = slots // LFRAMES
    has_up, has_down = t > 0, t < n_tile - 1
    inner = (t + n_tile - 1) // n_tile - (t + 1) // n_tile

    fetch = pltpu.make_async_copy(dest_hbm, dest_ref, dest_sem)
    fetch.start()
    barrier = pltpu.get_barrier_semaphore()

    def greet(group, tile):
        pl.semaphore_signal(barrier, inc=1, device_id=(group, tile), device_id_type=MESH)

    def in_line(k):
        return lax.rem(line + k, far) * low + place

    def in_row(k):
        return line * low + lax.rem(place + k, low)

    for k in range(far):
        for f in range(LFRAMES):
            source = f * half + t // 2
            if k > 0:
                greet(in_line(k), source)
            else:
                pl.when(source != t)(functools.partial(greet, g, source))
    for k in range(low):
        if k > 0:
            greet(in_row(k), t)
        pl.when(has_up)(functools.partial(greet, in_row(k), t - 1))
        pl.when(has_down)(functools.partial(greet, in_row(k), t + 1))

    zeros = jnp.zeros((low, LFRAMES, 3) + lat_ref.shape[1:], BF16)

    @pl.when(t == 0)
    def _():
        land[:, :, 0:3] = zeros

    @pl.when(t == n_tile - 1)
    def _():
        land[:, :, 3 + rows :] = zeros

    pl.semaphore_wait(barrier, 2 * far - 1 + inner + low * (2 + inner) - 1)

    frame = t // half
    first_tile = 2 * lax.rem(t, half)

    def one(k, h):
        return pltpu.make_async_remote_copy(
            src_ref=lat_ref.at[pl.ds(h * rows, rows)],
            dst_ref=held.at[line, frame],
            send_sem=send_sem.at[k, h],
            recv_sem=recv_sem.at[line, frame],
            device_id=(in_line(k), first_tile + h),
            device_id_type=MESH,
        )

    def own(h):
        return pltpu.make_async_copy(
            lat_ref.at[pl.ds(h * rows, rows)], held.at[line, frame], recv_sem.at[line, frame]
        )

    for k in list(range(1, far)) + [0]:
        for h in range(2):
            if k > 0:
                one(k, h).start()
            else:
                pl.when(first_tile + h != t)(lambda h=h: one(0, h).start())
                pl.when(first_tile + h == t)(lambda h=h: own(h).start())

    fetch.wait()
    per = slots * n_tile

    def source_of(group):
        found = jnp.int32(0)
        for j in range(n_req):
            found = jnp.where(dest_ref[j * per] // per == group, j, found)
        return found

    sources = [source_of(in_row(k)) for k in range(low)]

    for s in range(far):
        for f in range(LFRAMES):
            pltpu.make_async_copy(held.at[s, f], held.at[s, f], recv_sem.at[s, f]).wait()

    def two(k, n, src, dst, count, tile):
        return pltpu.make_async_remote_copy(
            src_ref=item.at[k, :, pl.ds(src, count)],
            dst_ref=land.at[place, :, pl.ds(dst, count)],
            send_sem=send_two.at[k, n],
            recv_sem=recv_two.at[place, n],
            device_id=(in_row(k), tile),
            device_id_type=MESH,
        )

    def across(k):
        return two(k, 0, 0, 3, rows, t)

    def up(k):
        return two(k, 1, 0, 3 + rows, 3, t - 1)

    def down(k):
        return two(k, 2, rows - 3, 0, 3, t + 1)

    def keep():
        return pltpu.make_async_copy(
            item.at[0], land.at[place, :, pl.ds(3, rows)], recv_two.at[place, 0]
        )

    for k in list(range(1, low)) + [0]:
        item[k] = held[sources[k] // low]
        if k > 0:
            across(k).start()
        else:
            keep().start()
        pl.when(has_up)(lambda k=k: up(k).start())
        pl.when(has_down)(lambda k=k: down(k).start())

    for k in range(far):
        for h in range(2):
            if k > 0:
                one(k, h).wait_send()
            else:
                pl.when(first_tile + h != t)(lambda h=h: one(0, h).wait_send())

    def landed(p, n, at, count):
        part = land.at[p, :, pl.ds(at, count)]
        pltpu.make_async_copy(part, part, recv_two.at[p, n]).wait()

    for p in range(low):
        landed(p, 0, 3, rows)
        pl.when(has_down)(functools.partial(landed, p, 1, 3 + rows, 3))
        pl.when(has_up)(functools.partial(landed, p, 2, 0, 3))

    out_ref[...] = land[lax.rem(sources[0], low)]

    for k in range(low):
        if k > 0:
            across(k).wait_send()
        pl.when(has_up)(lambda k=k: up(k).wait_send())
        pl.when(has_down)(lambda k=k: down(k).wait_send())


def route(n_req, n_tile, piece_dest, latents):
    slots, channels, cols = latents.shape
    rows = slots // LFRAMES
    far = n_req // 2 if n_req < 8 else 4
    low = n_req // far
    return pl.pallas_call(
        functools.partial(route_kernel, n_req, n_tile),
        out_shape=jax.ShapeDtypeStruct((LFRAMES, rows + 6, channels, cols), BF16),
        in_specs=[pl.BlockSpec(memory_space=pltpu.HBM)] * 2,
        out_specs=pl.BlockSpec(memory_space=pltpu.VMEM),
        scratch_shapes=[
            pltpu.SMEM(piece_dest.shape, jnp.int32),
            pltpu.VMEM((far, LFRAMES, rows, channels, cols), BF16),
            pltpu.VMEM((low, LFRAMES, rows, channels, cols), BF16),
            pltpu.VMEM((low, LFRAMES, rows + 6, channels, cols), BF16),
            pltpu.SemaphoreType.DMA,
            pltpu.SemaphoreType.DMA((far, 2)),
            pltpu.SemaphoreType.DMA((far, LFRAMES)),
            pltpu.SemaphoreType.DMA((low, 3)),
            pltpu.SemaphoreType.DMA((low, 3)),
        ],
        compiler_params=pltpu.CompilerParams(
            collective_id=0, has_side_effects=True, vmem_limit_bytes=VMEM_BYTES
        ),
        name="route",
    )(piece_dest, latents)


def shift(x, by):
    width = x.shape[1]
    lane = lax.broadcasted_iota(jnp.int32, x.shape, 1)
    if by == 1:
        return jnp.where(lane == 0, 0.0, pltpu.roll(x, 1, axis=1))
    return jnp.where(lane == width - 1, 0.0, pltpu.roll(x, width - 1, axis=1))


def column(ref):
    n = ref.shape[0]
    return jnp.transpose(jnp.broadcast_to(ref[...].reshape(1, n), (128, n)))


def decode_kernel(grid_ref, *refs):
    hbm, (out_ref, *refs) = refs[:12], refs[12:]
    frames_hbm, heights_hbm, widths_hbm, w_in_hbm = hbm[:4]
    vector_hbm, (w_res_hbm, w_time_hbm, w_up_hbm) = hbm[4:9], hbm[9:]
    frames_ref, heights_ref, widths_ref, *refs = refs
    vectors, refs = refs[:5], refs[5:]
    taps, w_in, wr, wt, wu_raw, wu, x_in, first, spread, timed, inter, result, perm, *refs = refs
    c_in, c_gain, c_res, c_time, c_up, sem_s, sem_v, sem_i, sem_r, sem_t, sem_u, sem_o = refs
    g = lax.axis_index("req")
    t = lax.axis_index("tile")
    channels, cols = grid_ref.shape[2], grid_ref.shape[3]
    rows = grid_ref.shape[1] - 6
    mid = taps.shape[1]
    outc = wu_raw.shape[2]
    one = 9 * channels
    mrows = rows + 4

    copies_s = [
        pltpu.make_async_copy(a, b, sem_s.at[i])
        for i, (a, b) in enumerate(
            zip((frames_hbm, heights_hbm, widths_hbm), (frames_ref, heights_ref, widths_ref))
        )
    ]
    copies_v = [
        pltpu.make_async_copy(a, b, sem_v.at[i])
        for i, (a, b) in enumerate(zip(vector_hbm, vectors))
    ]
    copies_i = [
        pltpu.make_async_copy(
            w_in_hbm.at[pl.ds((2 - i) * one, one)], taps.at[pl.ds(i * one, one)], sem_i.at[i]
        )
        for i in range(2)
    ]
    copies_r = []
    for d in range(3):
        for a in range(2):
            for e in range(3):
                copies_r.append(
                    pltpu.make_async_copy(
                        w_res_hbm.at[2 - a, d, e],
                        wr.at[pl.ds(a * mid, mid), pl.ds((d * 3 + e) * mid, mid)],
                        sem_r.at[d, a * 3 + e],
                    )
                )
    copies_t = [
        pltpu.make_async_copy(w_time_hbm.at[a + 1], wt.at[:, pl.ds(a * mid, mid)], sem_t.at[a])
        for a in range(2)
    ]
    copy_u = pltpu.make_async_copy(w_up_hbm, wu_raw, sem_u)
    for copy in copies_s + copies_v + copies_i + copies_r + copies_t + [copy_u]:
        copy.start()

    for copy in copies_s:
        copy.wait()
    src = lax.broadcasted_iota(jnp.int32, (2 * cols, 2 * cols), 0)
    dst = lax.broadcasted_iota(jnp.int32, (2 * cols, 2 * cols), 1)
    perm[...] = jnp.where(
        (src % cols == dst // 2) & (src // cols == dst % 2), 1.0, 0.0
    ).astype(BF16)

    n_frames, n_rows, n_cols = frames_ref[g], heights_ref[g], widths_ref[g]
    lane = lax.broadcasted_iota(jnp.int32, (1, cols), 1)

    def mask(f, r):
        live = (f < n_frames) & (r >= 0) & (r < n_rows)
        return lane < jnp.where(live, n_cols, 0)

    def masks(f, r, n):
        return jnp.concatenate([mask(f, r + i) for i in range(n)], axis=1)

    def wide(ref, n):
        return jnp.concatenate([ref[...]] * n, axis=1)

    for f in range(LFRAMES):
        base = (1 - f) * one
        for q in range(rows + 6):
            x = grid_ref[f, q].astype(F32)
            x = jnp.where(mask(f, rows * t - 3 + q), x, 0.0)
            for e, y in enumerate((shift(x, 1), x, shift(x, -1))):
                y = y.astype(BF16)
                for d in range(3):
                    if 0 <= q - d < mrows:
                        at = base + (d * 3 + e) * channels
                        x_in[at : at + channels, (q - d) * cols : (q - d + 1) * cols] = y

    for copy in copies_v + copies_i:
        copy.wait()
    w_in[...] = jnp.transpose(taps[...])
    for kept, vector in zip((c_in, c_gain, c_res, c_time, c_up), vectors):
        kept[...] = column(vector)

    span = mrows // 2

    def stage_first(p, carry):
        at = p * span * cols
        here = pl.ds(at, span * cols)
        for f in range(LFRAMES):
            if f == 0:
                x = x_in[one : 2 * one, here]
            else:
                x = x_in[:, here]
            acc = jnp.dot(w_in[:, 0 : x.shape[0]], x, preferred_element_type=F32)
            half = (acc + wide(c_in, span)).astype(BF16)
            first[f, :, here] = half
            v = half.astype(F32)
            mean = jnp.sum(v * v, axis=0, keepdims=True) * (1.0 / mid)
            v = v * lax.rsqrt(mean + 1e-06) * wide(c_gain, span)
            v = 0.5 * v * (1.0 + jnp.tanh(0.5 * v))
            v = jnp.where(masks(f, rows * t - 2 + span * p, span), v, 0.0)
            parts = [v[:, i * cols : (i + 1) * cols] for i in range(span)]
            for e in range(3):
                moved = parts if e == 1 else [shift(part, 1 - e) for part in parts]
                spread[(f * 3 + e) * mid : (f * 3 + e + 1) * mid, here] = jnp.concatenate(
                    moved, axis=1
                ).astype(BF16)
        return carry

    for p in range(2):
        stage_first(p, 0)

    for copy in copies_r + copies_t:
        copy.wait()

    brows = rows + 2
    taller = [
        jnp.concatenate(
            [
                spread[f * 3 * mid : (f + 1) * 3 * mid, d * cols : (d + brows) * cols]
                for d in range(3)
            ],
            axis=0,
        )
        for f in range(LFRAMES)
    ]
    old = jnp.dot(wr[...], taller[0], preferred_element_type=F32)
    new = jnp.dot(wr[0:mid], taller[1], preferred_element_type=F32)
    blocks = []
    for f, acc in enumerate((old[0:mid], old[mid:] + new)):
        kept = first[f, :, cols : (brows + 1) * cols].astype(F32)
        blocks.append((acc + wide(c_res, brows) + kept).astype(BF16))
    for f in range(LFRAMES):
        if f == 0:
            twice = jnp.dot(wt[:, mid:], blocks[0], preferred_element_type=F32)
        else:
            both = jnp.concatenate(blocks, axis=0)
            twice = jnp.dot(wt[...], both, preferred_element_type=F32)
        live = masks(f, rows * t - 1, brows)
        twice = jnp.where(live, twice + wide(c_time, brows), 0.0).astype(BF16)
        for k in range(2):
            timed[2 * f + k] = twice[k * mid : (k + 1) * mid]

    copy_u.wait()
    w0, w1, w2 = [wu_raw[d].reshape(3 * outc, mid) for d in range(3)]
    wu[0, :, 0:mid] = w0
    wu[0, :, mid:] = (w1.astype(F32) + w2.astype(F32)).astype(BF16)
    wu[1, :, 0:mid] = (w0.astype(F32) + w1.astype(F32)).astype(BF16)
    wu[1, :, mid:] = w2

    def stage_up(f, carry):
        x = [timed[f, :, i * cols : (i + rows) * cols] for i in range(3)]
        for k in range(2):
            z = jnp.dot(
                wu[k],
                jnp.concatenate([x[k], x[k + 1]], axis=0),
                preferred_element_type=F32,
            )
            for r in range(rows):
                z0, z1, z2 = [
                    z[e * outc : (e + 1) * outc, r * cols : (r + 1) * cols] for e in range(3)
                ]
                live = mask(f // 2, rows * t + r)
                base = z1 + c_up[...]
                even = jnp.where(live, shift(z0, 1) + z2 + base, 0.0)
                odd = jnp.where(live, z0 + shift(z2, -1) + base, 0.0)
                pair = jnp.concatenate([even, odd], axis=1).astype(BF16)
                row = jnp.dot(pair, perm[...], preferred_element_type=F32)
                for w in range(2):
                    inter[w, pl.ds(2 * r + k, outc, stride=2 * rows), :] = row[
                        :, w * cols : (w + 1) * cols
                    ]
        for w in range(2):
            result[f, :, :, w * cols : (w + 1) * cols] = (
                inter[w].reshape(outc, 2 * rows, cols).astype(BF16)
            )
        pltpu.make_async_copy(result.at[f], out_ref.at[0, :, f], sem_o.at[f]).start()
        return carry

    lax.fori_loop(0, 2 * LFRAMES, stage_up, 0, unroll=2)
    for f in range(2 * LFRAMES):
        pltpu.make_async_copy(result.at[f], out_ref.at[0, :, f], sem_o.at[f]).wait()


def decode(grid, frames, heights, widths, w_in, vectors, w_res, w_time, w_up):
    rows, cols = grid.shape[1] - 6, grid.shape[3]
    channels = grid.shape[2]
    mid, outc = w_res.shape[3], w_up.shape[2]
    vmem = pl.BlockSpec(memory_space=pltpu.VMEM)
    return pl.pallas_call(
        decode_kernel,
        out_shape=jax.ShapeDtypeStruct((1, outc, 2 * LFRAMES, 2 * rows, 2 * cols), BF16),
        in_specs=[vmem] + [pl.BlockSpec(memory_space=pltpu.HBM)] * 12,
        out_specs=pl.BlockSpec(memory_space=pltpu.HBM),
        scratch_shapes=[pltpu.SMEM(v.shape, jnp.int32) for v in (frames, heights, widths)]
        + [pltpu.VMEM(v.shape, F32) for v in vectors]
        + [
            pltpu.VMEM((18 * channels, mid), BF16),
            pltpu.VMEM((mid, 18 * channels), BF16),
            pltpu.VMEM((2 * mid, 9 * mid), BF16),
            pltpu.VMEM((2 * mid, 2 * mid), BF16),
            pltpu.VMEM(w_up.shape, BF16),
            pltpu.VMEM((2, 3 * outc, 2 * mid), BF16),
            pltpu.VMEM((18 * channels, (rows + 4) * cols), BF16),
            pltpu.VMEM((LFRAMES, mid, (rows + 4) * cols), BF16),
            pltpu.VMEM((6 * mid, (rows + 4) * cols), BF16),
            pltpu.VMEM((2 * LFRAMES, mid, (rows + 2) * cols), BF16),
            pltpu.VMEM((2, outc * 2 * rows, cols), F32),
            pltpu.VMEM((2 * LFRAMES, outc, 2 * rows, 2 * cols), BF16),
            pltpu.VMEM((2 * cols, 2 * cols), BF16),
            pltpu.VMEM((mid, 128), F32),
            pltpu.VMEM((mid, 128), F32),
            pltpu.VMEM((mid, 128), F32),
            pltpu.VMEM((2 * mid, 128), F32),
            pltpu.VMEM((outc, 128), F32),
            pltpu.SemaphoreType.DMA((3,)),
            pltpu.SemaphoreType.DMA((5,)),
            pltpu.SemaphoreType.DMA((2,)),
            pltpu.SemaphoreType.DMA((3, 6)),
            pltpu.SemaphoreType.DMA((2,)),
            pltpu.SemaphoreType.DMA,
            pltpu.SemaphoreType.DMA((2 * LFRAMES,)),
        ],
        compiler_params=pltpu.CompilerParams(vmem_limit_bytes=VMEM_BYTES),
        name="decode",
    )(grid, frames, heights, widths, w_in, *vectors, w_res, w_time, w_up)


def solution(mesh):
    n_req, n_tile = mesh.shape["req"], mesh.shape["tile"]

    def on_device(
        latents, piece_dest, frames, heights, widths,
        w_in, b_in, gain_norm, w_res, b_res, w_time, b_time, w_up, b_up,
    ):
        grid = route(n_req, n_tile, piece_dest, latents)
        mid, channels = w_in.shape[3], w_in.shape[4]
        taps = jnp.transpose(w_in, (0, 1, 2, 4, 3)).reshape(27 * channels, mid)
        vectors = (b_in, gain_norm, b_res, b_time, b_up)
        return decode(grid, frames, heights, widths, taps, vectors, w_res, w_time, w_up)

    return jax.shard_map(
        on_device,
        mesh=mesh,
        in_specs=(P(("req", "tile"), None, None),) + (P(),) * 13,
        out_specs=P("req", None, None, "tile", None),
        check_vma=False,
    )
```

```python
import functools

import jax
import jax.numpy as jnp
from jax import lax
from jax.experimental import pallas as pl
from jax.experimental.pallas import tpu as pltpu
from jax.sharding import PartitionSpec as P

LFRAMES = 2
MESH = pl.DeviceIdType.MESH
VMEM_BYTES = 63 * 2**20
F32 = jnp.float32
BF16 = jnp.bfloat16


def route_kernel(
    n_req, n_tile, dest_hbm, lat_ref, out_ref,
    dest_ref, held, item, land, dest_sem, send_sem, recv_sem, send_two, recv_two,
):
    g = lax.axis_index("req")
    t = lax.axis_index("tile")
    far = n_req // 2 if n_req < 8 else 4
    low = n_req // far
    line, place = g // low, lax.rem(g, low)
    half = n_tile // 2
    slots = lat_ref.shape[0]
    rows = slots // LFRAMES
    has_up, has_down = t > 0, t < n_tile - 1
    inner = (t + n_tile - 1) // n_tile - (t + 1) // n_tile

    fetch = pltpu.make_async_copy(dest_hbm, dest_ref, dest_sem)
    fetch.start()
    barrier = pltpu.get_barrier_semaphore()

    def greet(group, tile):
        pl.semaphore_signal(barrier, inc=1, device_id=(group, tile), device_id_type=MESH)

    def in_line(k):
        return lax.rem(line + k, far) * low + place

    def in_row(k):
        return line * low + lax.rem(place + k, low)

    for k in range(far):
        for f in range(LFRAMES):
            source = f * half + t // 2
            if k > 0:
                greet(in_line(k), source)
            else:
                pl.when(source != t)(functools.partial(greet, g, source))
    for k in range(low):
        if k > 0:
            greet(in_row(k), t)
        pl.when(has_up)(functools.partial(greet, in_row(k), t - 1))
        pl.when(has_down)(functools.partial(greet, in_row(k), t + 1))

    zeros = jnp.zeros((low, LFRAMES, 3) + lat_ref.shape[1:], BF16)

    @pl.when(t == 0)
    def _():
        land[:, :, 0:3] = zeros

    @pl.when(t == n_tile - 1)
    def _():
        land[:, :, 3 + rows :] = zeros

    pl.semaphore_wait(barrier, 2 * far - 1 + inner + low * (2 + inner) - 1)

    frame = t // half
    first_tile = 2 * lax.rem(t, half)

    def one(k, h):
        return pltpu.make_async_remote_copy(
            src_ref=lat_ref.at[pl.ds(h * rows, rows)],
            dst_ref=held.at[line, frame],
            send_sem=send_sem.at[k, h],
            recv_sem=recv_sem.at[line, frame],
            device_id=(in_line(k), first_tile + h),
            device_id_type=MESH,
        )

    def own(h):
        return pltpu.make_async_copy(
            lat_ref.at[pl.ds(h * rows, rows)], held.at[line, frame], recv_sem.at[line, frame]
        )

    for k in list(range(1, far)) + [0]:
        for h in range(2):
            if k > 0:
                one(k, h).start()
            else:
                pl.when(first_tile + h != t)(lambda h=h: one(0, h).start())
                pl.when(first_tile + h == t)(lambda h=h: own(h).start())

    fetch.wait()
    per = slots * n_tile

    def source_of(group):
        found = jnp.int32(0)
        for j in range(n_req):
            found = jnp.where(dest_ref[j * per] // per == group, j, found)
        return found

    sources = [source_of(in_row(k)) for k in range(low)]

    for s in range(far):
        for f in range(LFRAMES):
            pltpu.make_async_copy(held.at[s, f], held.at[s, f], recv_sem.at[s, f]).wait()

    def two(k, n, src, dst, count, tile):
        return pltpu.make_async_remote_copy(
            src_ref=item.at[k, :, pl.ds(src, count)],
            dst_ref=land.at[place, :, pl.ds(dst, count)],
            send_sem=send_two.at[k, n],
            recv_sem=recv_two.at[place, n],
            device_id=(in_row(k), tile),
            device_id_type=MESH,
        )

    def across(k):
        return two(k, 0, 0, 3, rows, t)

    def up(k):
        return two(k, 1, 0, 3 + rows, 3, t - 1)

    def down(k):
        return two(k, 2, rows - 3, 0, 3, t + 1)

    def keep():
        return pltpu.make_async_copy(
            item.at[0], land.at[place, :, pl.ds(3, rows)], recv_two.at[place, 0]
        )

    for k in list(range(1, low)) + [0]:
        item[k] = held[sources[k] // low]
        if k > 0:
            across(k).start()
        else:
            keep().start()
        pl.when(has_up)(lambda k=k: up(k).start())
        pl.when(has_down)(lambda k=k: down(k).start())

    for k in range(far):
        for h in range(2):
            if k > 0:
                one(k, h).wait_send()
            else:
                pl.when(first_tile + h != t)(lambda h=h: one(0, h).wait_send())

    def landed(p, n, at, count):
        part = land.at[p, :, pl.ds(at, count)]
        pltpu.make_async_copy(part, part, recv_two.at[p, n]).wait()

    for p in range(low):
        landed(p, 0, 3, rows)
        pl.when(has_down)(functools.partial(landed, p, 1, 3 + rows, 3))
        pl.when(has_up)(functools.partial(landed, p, 2, 0, 3))

    out_ref[...] = land[lax.rem(sources[0], low)]

    for k in range(low):
        if k > 0:
            across(k).wait_send()
        pl.when(has_up)(lambda k=k: up(k).wait_send())
        pl.when(has_down)(lambda k=k: down(k).wait_send())


def route(n_req, n_tile, piece_dest, latents):
    slots, channels, cols = latents.shape
    rows = slots // LFRAMES
    far = n_req // 2 if n_req < 8 else 4
    low = n_req // far
    return pl.pallas_call(
        functools.partial(route_kernel, n_req, n_tile),
        out_shape=jax.ShapeDtypeStruct((LFRAMES, rows + 6, channels, cols), BF16),
        in_specs=[pl.BlockSpec(memory_space=pltpu.HBM)] * 2,
        out_specs=pl.BlockSpec(memory_space=pltpu.VMEM),
        scratch_shapes=[
            pltpu.SMEM(piece_dest.shape, jnp.int32),
            pltpu.VMEM((far, LFRAMES, rows, channels, cols), BF16),
            pltpu.VMEM((low, LFRAMES, rows, channels, cols), BF16),
            pltpu.VMEM((low, LFRAMES, rows + 6, channels, cols), BF16),
            pltpu.SemaphoreType.DMA,
            pltpu.SemaphoreType.DMA((far, 2)),
            pltpu.SemaphoreType.DMA((far, LFRAMES)),
            pltpu.SemaphoreType.DMA((low, 3)),
            pltpu.SemaphoreType.DMA((low, 3)),
        ],
        compiler_params=pltpu.CompilerParams(
            collective_id=0, has_side_effects=True, vmem_limit_bytes=VMEM_BYTES
        ),
        name="route",
    )(piece_dest, latents)


def shift(x, by):
    width = x.shape[1]
    lane = lax.broadcasted_iota(jnp.int32, x.shape, 1)
    if by == 1:
        return jnp.where(lane == 0, 0.0, pltpu.roll(x, 1, axis=1))
    return jnp.where(lane == width - 1, 0.0, pltpu.roll(x, width - 1, axis=1))


def column(ref):
    n = ref.shape[0]
    return jnp.transpose(jnp.broadcast_to(ref[...].reshape(1, n), (128, n)))


def decode_kernel(grid_ref, *refs):
    hbm, (out_ref, *refs) = refs[:12], refs[12:]
    frames_hbm, heights_hbm, widths_hbm, w_in_hbm = hbm[:4]
    vector_hbm, (w_res_hbm, w_time_hbm, w_up_hbm) = hbm[4:9], hbm[9:]
    frames_ref, heights_ref, widths_ref, *refs = refs
    vectors, refs = refs[:5], refs[5:]
    taps, w_in, wr, wt, wu_raw, wu, x_in, first, spread, timed, inter, result, perm, *refs = refs
    c_in, c_gain, c_res, c_time, c_up, sem_s, sem_v, sem_i, sem_r, sem_t, sem_u, sem_o = refs
    g = lax.axis_index("req")
    t = lax.axis_index("tile")
    channels, cols = grid_ref.shape[2], grid_ref.shape[3]
    rows = grid_ref.shape[1] - 6
    mid = taps.shape[1]
    outc = wu_raw.shape[2]
    one = 9 * channels
    mrows = rows + 4

    copies_s = [
        pltpu.make_async_copy(a, b, sem_s.at[i])
        for i, (a, b) in enumerate(
            zip((frames_hbm, heights_hbm, widths_hbm), (frames_ref, heights_ref, widths_ref))
        )
    ]
    copies_v = [
        pltpu.make_async_copy(a, b, sem_v.at[i])
        for i, (a, b) in enumerate(zip(vector_hbm, vectors))
    ]
    copies_i = [
        pltpu.make_async_copy(
            w_in_hbm.at[pl.ds((2 - i) * one, one)], taps.at[pl.ds(i * one, one)], sem_i.at[i]
        )
        for i in range(2)
    ]
    copies_r = []
    for d in range(3):
        for a in range(2):
            for e in range(3):
                copies_r.append(
                    pltpu.make_async_copy(
                        w_res_hbm.at[2 - a, d, e],
                        wr.at[pl.ds(a * mid, mid), pl.ds((d * 3 + e) * mid, mid)],
                        sem_r.at[d, a * 3 + e],
                    )
                )
    copies_t = [
        pltpu.make_async_copy(w_time_hbm.at[a + 1], wt.at[:, pl.ds(a * mid, mid)], sem_t.at[a])
        for a in range(2)
    ]
    copy_u = pltpu.make_async_copy(w_up_hbm, wu_raw, sem_u)
    for copy in copies_s + copies_v + copies_i + copies_r + copies_t + [copy_u]:
        copy.start()

    for copy in copies_s:
        copy.wait()
    n_frames, n_rows, n_cols = frames_ref[g], heights_ref[g], widths_ref[g]
    lane = lax.broadcasted_iota(jnp.int32, (1, cols), 1)

    def mask(f, r):
        live = (f < n_frames) & (r >= 0) & (r < n_rows)
        return lane < jnp.where(live, n_cols, 0)

    src = lax.broadcasted_iota(jnp.int32, (2 * cols, 2 * cols), 0)
    dst = lax.broadcasted_iota(jnp.int32, (2 * cols, 2 * cols), 1)
    pick = (src % cols == dst // 2) & (src // cols == dst % 2) & (dst // 2 < n_cols)
    perm[0] = jnp.where(pick, 1.0, 0.0).astype(BF16)
    perm[1] = jnp.zeros((2 * cols, 2 * cols), BF16)

    def masks(f, r, n):
        return jnp.concatenate([mask(f, r + i) for i in range(n)], axis=1)

    def wide(ref, n):
        return jnp.concatenate([ref[...]] * n, axis=1)

    for f in range(LFRAMES):
        base = (1 - f) * one
        for q in range(rows + 6):
            x = grid_ref[f, q].astype(F32)
            x = jnp.where(mask(f, rows * t - 3 + q), x, 0.0)
            for e, y in enumerate((shift(x, 1), x, shift(x, -1))):
                y = y.astype(BF16)
                for d in range(3):
                    if 0 <= q - d < mrows:
                        at = base + (d * 3 + e) * channels
                        x_in[at : at + channels, (q - d) * cols : (q - d + 1) * cols] = y

    for copy in copies_v + copies_i:
        copy.wait()
    w_in[...] = jnp.transpose(taps[...])
    for kept, vector in zip((c_in, c_gain, c_res, c_time, c_up), vectors):
        kept[...] = column(vector)

    span = mrows // 2

    def stage_first(f, p):
        at = p * span * cols
        here = pl.ds(at, span * cols)
        x = x_in[one : 2 * one, here] if f == 0 else x_in[:, here]
        acc = jnp.dot(w_in[:, 0 : x.shape[0]], x, preferred_element_type=F32)
        half = (acc + wide(c_in, span)).astype(BF16)
        first[f, :, here] = half
        v = half.astype(F32)
        mean = jnp.sum(v * v, axis=0, keepdims=True) * (1.0 / mid)
        v = v * lax.rsqrt(mean + 1e-06) * wide(c_gain, span)
        v = 0.5 * v * (1.0 + jnp.tanh(0.5 * v))
        v = jnp.where(masks(f, rows * t - 2 + span * p, span), v, 0.0)
        parts = [v[:, i * cols : (i + 1) * cols] for i in range(span)]
        for e in range(3):
            moved = parts if e == 1 else [shift(part, 1 - e) for part in parts]
            spread[(f * 3 + e) * mid : (f * 3 + e + 1) * mid, here] = jnp.concatenate(
                moved, axis=1
            ).astype(BF16)

    brows = rows + 2

    def taller(f):
        return jnp.concatenate(
            [
                spread[f * 3 * mid : (f + 1) * 3 * mid, d * cols : (d + brows) * cols]
                for d in range(3)
            ],
            axis=0,
        )

    def stage_block(f, acc):
        kept = first[f, :, cols : (brows + 1) * cols].astype(F32)
        return (acc + wide(c_res, brows) + kept).astype(BF16)

    def stage_time(f, x):
        twice = jnp.dot(wt[:, 2 * mid - x.shape[0] :], x, preferred_element_type=F32)
        live = masks(f, rows * t - 1, brows)
        twice = jnp.where(live, twice + wide(c_time, brows), 0.0).astype(BF16)
        for k in range(2):
            timed[2 * f + k] = twice[k * mid : (k + 1) * mid]

    def stage_up(f):
        x = [timed[f, :, i * cols : (i + rows) * cols] for i in range(3)]
        for k in range(2):
            z = jnp.dot(
                wu[k],
                jnp.concatenate([x[k], x[k + 1]], axis=0),
                preferred_element_type=F32,
            )
            for r in range(rows):
                z0, z1, z2 = [
                    z[e * outc : (e + 1) * outc, r * cols : (r + 1) * cols] for e in range(3)
                ]
                live = (f // 2 < n_frames) & (rows * t + r < n_rows)
                base = z1 + c_up[...]
                even = (shift(z0, 1) + z2 + base).astype(BF16)
                odd = (z0 + shift(z2, -1) + base).astype(BF16)
                pair = jnp.concatenate([even, odd], axis=1)
                row = jnp.dot(pair, perm[jnp.where(live, 0, 1)], preferred_element_type=F32)
                for w in range(2):
                    inter[f % 2, w, pl.ds(2 * r + k, outc, stride=2 * rows), :] = row[
                        :, w * cols : (w + 1) * cols
                    ]
        for w in range(2):
            result[f, :, :, w * cols : (w + 1) * cols] = (
                inter[f % 2, w].reshape(outc, 2 * rows, cols).astype(BF16)
            )
        pltpu.make_async_copy(result.at[f], out_ref.at[0, :, f], sem_o.at[f]).start()


    for p in range(2):
        stage_first(0, p)
    for copy in copies_r + copies_t + [copy_u]:
        copy.wait()
    old = jnp.dot(wr[...], taller(0), preferred_element_type=F32)
    for p in range(2):
        stage_first(1, p)
    w0, w1, w2 = [wu_raw[d].reshape(3 * outc, mid) for d in range(3)]
    wu[0, :, 0:mid] = w0
    wu[0, :, mid:] = (w1.astype(F32) + w2.astype(F32)).astype(BF16)
    wu[1, :, 0:mid] = (w0.astype(F32) + w1.astype(F32)).astype(BF16)
    wu[1, :, mid:] = w2

    block0 = stage_block(0, old[0:mid])
    stage_time(0, block0)
    new = jnp.dot(wr[0:mid], taller(1), preferred_element_type=F32)
    stage_up(0)
    block1 = stage_block(1, old[mid:] + new)
    stage_time(1, jnp.concatenate([block0, block1], axis=0))
    for f in range(1, 2 * LFRAMES):
        stage_up(f)
    for f in range(2 * LFRAMES):
        pltpu.make_async_copy(result.at[f], out_ref.at[0, :, f], sem_o.at[f]).wait()


def decode(grid, frames, heights, widths, w_in, vectors, w_res, w_time, w_up):
    rows, cols = grid.shape[1] - 6, grid.shape[3]
    channels = grid.shape[2]
    mid, outc = w_res.shape[3], w_up.shape[2]
    vmem = pl.BlockSpec(memory_space=pltpu.VMEM)
    return pl.pallas_call(
        decode_kernel,
        out_shape=jax.ShapeDtypeStruct((1, outc, 2 * LFRAMES, 2 * rows, 2 * cols), BF16),
        in_specs=[vmem] + [pl.BlockSpec(memory_space=pltpu.HBM)] * 12,
        out_specs=pl.BlockSpec(memory_space=pltpu.HBM),
        scratch_shapes=[pltpu.SMEM(v.shape, jnp.int32) for v in (frames, heights, widths)]
        + [pltpu.VMEM(v.shape, F32) for v in vectors]
        + [
            pltpu.VMEM((18 * channels, mid), BF16),
            pltpu.VMEM((mid, 18 * channels), BF16),
            pltpu.VMEM((2 * mid, 9 * mid), BF16),
            pltpu.VMEM((2 * mid, 2 * mid), BF16),
            pltpu.VMEM(w_up.shape, BF16),
            pltpu.VMEM((2, 3 * outc, 2 * mid), BF16),
            pltpu.VMEM((18 * channels, (rows + 4) * cols), BF16),
            pltpu.VMEM((LFRAMES, mid, (rows + 4) * cols), BF16),
            pltpu.VMEM((6 * mid, (rows + 4) * cols), BF16),
            pltpu.VMEM((2 * LFRAMES, mid, (rows + 2) * cols), BF16),
            pltpu.VMEM((2, 2, outc * 2 * rows, cols), F32),
            pltpu.VMEM((2 * LFRAMES, outc, 2 * rows, 2 * cols), BF16),
            pltpu.VMEM((2, 2 * cols, 2 * cols), BF16),
            pltpu.VMEM((mid, 128), F32),
            pltpu.VMEM((mid, 128), F32),
            pltpu.VMEM((mid, 128), F32),
            pltpu.VMEM((2 * mid, 128), F32),
            pltpu.VMEM((outc, 128), F32),
            pltpu.SemaphoreType.DMA((3,)),
            pltpu.SemaphoreType.DMA((5,)),
            pltpu.SemaphoreType.DMA((2,)),
            pltpu.SemaphoreType.DMA((3, 6)),
            pltpu.SemaphoreType.DMA((2,)),
            pltpu.SemaphoreType.DMA,
            pltpu.SemaphoreType.DMA((2 * LFRAMES,)),
        ],
        compiler_params=pltpu.CompilerParams(vmem_limit_bytes=VMEM_BYTES),
        name="decode",
    )(grid, frames, heights, widths, w_in, *vectors, w_res, w_time, w_up)


def solution(mesh):
    n_req, n_tile = mesh.shape["req"], mesh.shape["tile"]

    def on_device(
        latents, piece_dest, frames, heights, widths,
        w_in, b_in, gain_norm, w_res, b_res, w_time, b_time, w_up, b_up,
    ):
        grid = route(n_req, n_tile, piece_dest, latents)
        mid, channels = w_in.shape[3], w_in.shape[4]
        taps = jnp.transpose(w_in, (0, 1, 2, 4, 3)).reshape(27 * channels, mid)
        vectors = (b_in, gain_norm, b_res, b_time, b_up)
        return decode(grid, frames, heights, widths, taps, vectors, w_res, w_time, w_up)

    return jax.shard_map(
        on_device,
        mesh=mesh,
        in_specs=(P(("req", "tile"), None, None),) + (P(),) * 13,
        out_specs=P("req", None, None, "tile", None),
        check_vma=False,
    )
```

```python
import functools

import jax
import jax.numpy as jnp
from jax import lax
from jax.experimental import pallas as pl
from jax.experimental.pallas import tpu as pltpu
from jax.sharding import PartitionSpec as P

LFRAMES = 2
MESH = pl.DeviceIdType.MESH
VMEM_BYTES = 63 * 2**20
F32 = jnp.float32
BF16 = jnp.bfloat16


def route_kernel(
    n_req, n_tile, dest_hbm, lat_ref, out_ref,
    dest_ref, held, item, land, dest_sem, send_sem, recv_sem, send_two, recv_two,
):
    g = lax.axis_index("req")
    t = lax.axis_index("tile")
    far = n_req // 2 if n_req < 8 else 4
    low = n_req // far
    line, place = g // low, lax.rem(g, low)
    half = n_tile // 2
    slots = lat_ref.shape[0]
    rows = slots // LFRAMES
    has_up, has_down = t > 0, t < n_tile - 1
    inner = (t + n_tile - 1) // n_tile - (t + 1) // n_tile

    fetch = pltpu.make_async_copy(dest_hbm, dest_ref, dest_sem)
    fetch.start()
    barrier = pltpu.get_barrier_semaphore()

    def greet(group, tile):
        pl.semaphore_signal(barrier, inc=1, device_id=(group, tile), device_id_type=MESH)

    def in_line(k):
        return lax.rem(line + k, far) * low + place

    def in_row(k):
        return line * low + lax.rem(place + k, low)

    for k in range(far):
        for f in range(LFRAMES):
            source = f * half + t // 2
            if k > 0:
                greet(in_line(k), source)
            else:
                pl.when(source != t)(functools.partial(greet, g, source))
    for k in range(low):
        if k > 0:
            greet(in_row(k), t)
        pl.when(has_up)(functools.partial(greet, in_row(k), t - 1))
        pl.when(has_down)(functools.partial(greet, in_row(k), t + 1))

    zeros = jnp.zeros((low, LFRAMES, 3) + lat_ref.shape[1:], BF16)

    @pl.when(t == 0)
    def _():
        land[:, :, 0:3] = zeros

    @pl.when(t == n_tile - 1)
    def _():
        land[:, :, 3 + rows :] = zeros

    pl.semaphore_wait(barrier, 2 * far - 1 + inner + low * (2 + inner) - 1)

    frame = t // half
    first_tile = 2 * lax.rem(t, half)

    def one(k, h):
        return pltpu.make_async_remote_copy(
            src_ref=lat_ref.at[pl.ds(h * rows, rows)],
            dst_ref=held.at[line, frame],
            send_sem=send_sem.at[k, h],
            recv_sem=recv_sem.at[line, frame],
            device_id=(in_line(k), first_tile + h),
            device_id_type=MESH,
        )

    def own(h):
        return pltpu.make_async_copy(
            lat_ref.at[pl.ds(h * rows, rows)], held.at[line, frame], recv_sem.at[line, frame]
        )

    for k in list(range(1, far)) + [0]:
        for h in range(2):
            if k > 0:
                one(k, h).start()
            else:
                pl.when(first_tile + h != t)(lambda h=h: one(0, h).start())
                pl.when(first_tile + h == t)(lambda h=h: own(h).start())

    fetch.wait()
    per = slots * n_tile

    def source_of(group):
        found = jnp.int32(0)
        for j in range(n_req):
            found = jnp.where(dest_ref[j * per] // per == group, j, found)
        return found

    sources = [source_of(in_row(k)) for k in range(low)]

    for s in range(far):
        for f in range(LFRAMES):
            pltpu.make_async_copy(held.at[s, f], held.at[s, f], recv_sem.at[s, f]).wait()

    def two(k, n, src, dst, count, tile):
        return pltpu.make_async_remote_copy(
            src_ref=item.at[k, :, pl.ds(src, count)],
            dst_ref=land.at[place, :, pl.ds(dst, count)],
            send_sem=send_two.at[k, n],
            recv_sem=recv_two.at[place, n],
            device_id=(in_row(k), tile),
            device_id_type=MESH,
        )

    def across(k):
        return two(k, 0, 0, 3, rows, t)

    def up(k):
        return two(k, 1, 0, 3 + rows, 3, t - 1)

    def down(k):
        return two(k, 2, rows - 3, 0, 3, t + 1)

    def keep():
        return pltpu.make_async_copy(
            item.at[0], land.at[place, :, pl.ds(3, rows)], recv_two.at[place, 0]
        )

    for k in list(range(1, low)) + [0]:
        item[k] = held[sources[k] // low]
        if k > 0:
            across(k).start()
        else:
            keep().start()
        pl.when(has_up)(lambda k=k: up(k).start())
        pl.when(has_down)(lambda k=k: down(k).start())

    for k in range(far):
        for h in range(2):
            if k > 0:
                one(k, h).wait_send()
            else:
                pl.when(first_tile + h != t)(lambda h=h: one(0, h).wait_send())

    def landed(p, n, at, count):
        part = land.at[p, :, pl.ds(at, count)]
        pltpu.make_async_copy(part, part, recv_two.at[p, n]).wait()

    for p in range(low):
        landed(p, 0, 3, rows)
        pl.when(has_down)(functools.partial(landed, p, 1, 3 + rows, 3))
        pl.when(has_up)(functools.partial(landed, p, 2, 0, 3))

    out_ref[...] = land[lax.rem(sources[0], low)]

    for k in range(low):
        if k > 0:
            across(k).wait_send()
        pl.when(has_up)(lambda k=k: up(k).wait_send())
        pl.when(has_down)(lambda k=k: down(k).wait_send())


def route(n_req, n_tile, piece_dest, latents):
    slots, channels, cols = latents.shape
    rows = slots // LFRAMES
    far = n_req // 2 if n_req < 8 else 4
    low = n_req // far
    return pl.pallas_call(
        functools.partial(route_kernel, n_req, n_tile),
        out_shape=jax.ShapeDtypeStruct((LFRAMES, rows + 6, channels, cols), BF16),
        in_specs=[pl.BlockSpec(memory_space=pltpu.HBM)] * 2,
        out_specs=pl.BlockSpec(memory_space=pltpu.VMEM),
        scratch_shapes=[
            pltpu.SMEM(piece_dest.shape, jnp.int32),
            pltpu.VMEM((far, LFRAMES, rows, channels, cols), BF16),
            pltpu.VMEM((low, LFRAMES, rows, channels, cols), BF16),
            pltpu.VMEM((low, LFRAMES, rows + 6, channels, cols), BF16),
            pltpu.SemaphoreType.DMA,
            pltpu.SemaphoreType.DMA((far, 2)),
            pltpu.SemaphoreType.DMA((far, LFRAMES)),
            pltpu.SemaphoreType.DMA((low, 3)),
            pltpu.SemaphoreType.DMA((low, 3)),
        ],
        compiler_params=pltpu.CompilerParams(
            collective_id=0, has_side_effects=True, vmem_limit_bytes=VMEM_BYTES
        ),
        name="route",
    )(piece_dest, latents)


def shift(x, by):
    width = x.shape[1]
    lane = lax.broadcasted_iota(jnp.int32, x.shape, 1)
    if by == 1:
        return jnp.where(lane == 0, 0.0, pltpu.roll(x, 1, axis=1))
    return jnp.where(lane == width - 1, 0.0, pltpu.roll(x, width - 1, axis=1))


def column(ref):
    n = ref.shape[0]
    return jnp.transpose(jnp.broadcast_to(ref[...].reshape(1, n), (128, n)))


def decode_kernel(grid_ref, *refs):
    hbm, (out_ref, *refs) = refs[:12], refs[12:]
    frames_hbm, heights_hbm, widths_hbm, w_in_hbm = hbm[:4]
    vector_hbm, (w_res_hbm, w_time_hbm, w_up_hbm) = hbm[4:9], hbm[9:]
    frames_ref, heights_ref, widths_ref, *refs = refs
    vectors, refs = refs[:5], refs[5:]
    taps, w_in, wr, wt, wu_raw, wu, x_in, first, spread, timed, result, perm, *refs = refs
    c_in, c_gain, c_res, c_time, c_up, sem_s, sem_v, sem_i, sem_r, sem_t, sem_u, sem_o = refs
    g = lax.axis_index("req")
    t = lax.axis_index("tile")
    channels, cols = grid_ref.shape[2], grid_ref.shape[3]
    rows = grid_ref.shape[1] - 6
    mid = taps.shape[1]
    outc = wu_raw.shape[2]
    one = 9 * channels
    mrows = rows + 4

    copies_s = [
        pltpu.make_async_copy(a, b, sem_s.at[i])
        for i, (a, b) in enumerate(
            zip((frames_hbm, heights_hbm, widths_hbm), (frames_ref, heights_ref, widths_ref))
        )
    ]
    copies_v = [
        pltpu.make_async_copy(a, b, sem_v.at[i])
        for i, (a, b) in enumerate(zip(vector_hbm, vectors))
    ]
    copies_i = [
        pltpu.make_async_copy(
            w_in_hbm.at[pl.ds((2 - i) * one, one)], taps.at[pl.ds(i * one, one)], sem_i.at[i]
        )
        for i in range(2)
    ]
    copies_r = []
    for d in range(3):
        for a in range(2):
            for e in range(3):
                copies_r.append(
                    pltpu.make_async_copy(
                        w_res_hbm.at[2 - a, d, e],
                        wr.at[pl.ds(a * mid, mid), pl.ds((d * 3 + e) * mid, mid)],
                        sem_r.at[d, a * 3 + e],
                    )
                )
    copies_t = [
        pltpu.make_async_copy(w_time_hbm.at[a + 1], wt.at[:, pl.ds(a * mid, mid)], sem_t.at[a])
        for a in range(2)
    ]
    copy_u = pltpu.make_async_copy(w_up_hbm, wu_raw, sem_u)
    for copy in copies_s + copies_v + copies_i + copies_r + copies_t + [copy_u]:
        copy.start()

    for copy in copies_s:
        copy.wait()
    n_frames, n_rows, n_cols = frames_ref[g], heights_ref[g], widths_ref[g]
    lane = lax.broadcasted_iota(jnp.int32, (1, cols), 1)

    def mask(f, r):
        live = (f < n_frames) & (r >= 0) & (r < n_rows)
        return lane < jnp.where(live, n_cols, 0)

    src = lax.broadcasted_iota(jnp.int32, (2 * cols, 2 * cols), 0)
    dst = lax.broadcasted_iota(jnp.int32, (2 * cols, 2 * cols), 1)
    pick = (src % cols == dst // 2) & (src // cols == dst % 2) & (dst // 2 < n_cols)
    perm[...] = jnp.where(pick, 1.0, 0.0).astype(BF16)

    def masks(f, r, n):
        return jnp.concatenate([mask(f, r + i) for i in range(n)], axis=1)

    def wide(ref, n):
        return jnp.concatenate([ref[...]] * n, axis=1)

    for f in range(LFRAMES):
        base = (1 - f) * one
        for q in range(rows + 6):
            x = grid_ref[f, q].astype(F32)
            x = jnp.where(mask(f, rows * t - 3 + q), x, 0.0)
            for e, y in enumerate((shift(x, 1), x, shift(x, -1))):
                y = y.astype(BF16)
                for d in range(3):
                    if 0 <= q - d < mrows:
                        at = base + (d * 3 + e) * channels
                        x_in[at : at + channels, (q - d) * cols : (q - d + 1) * cols] = y

    for copy in copies_v + copies_i:
        copy.wait()
    w_in[...] = jnp.transpose(taps[...])
    for kept, vector in zip((c_in, c_gain, c_res, c_time, c_up), vectors):
        kept[...] = column(vector)

    span = mrows // 2

    def stage_first(f, p):
        at = p * span * cols
        here = pl.ds(at, span * cols)
        x = x_in[one : 2 * one, here] if f == 0 else x_in[:, here]
        acc = jnp.dot(w_in[:, 0 : x.shape[0]], x, preferred_element_type=F32)
        half = (acc + wide(c_in, span)).astype(BF16)
        first[f, :, here] = half
        v = half.astype(F32)
        mean = jnp.sum(v * v, axis=0, keepdims=True) * (1.0 / mid)
        v = v * lax.rsqrt(mean + 1e-06) * wide(c_gain, span)
        v = 0.5 * v * (1.0 + jnp.tanh(0.5 * v))
        v = jnp.where(masks(f, rows * t - 2 + span * p, span), v, 0.0)
        parts = [v[:, i * cols : (i + 1) * cols] for i in range(span)]
        for e in range(3):
            moved = parts if e == 1 else [shift(part, 1 - e) for part in parts]
            spread[(f * 3 + e) * mid : (f * 3 + e + 1) * mid, here] = jnp.concatenate(
                moved, axis=1
            ).astype(BF16)

    brows = rows + 2

    def taller(f):
        return jnp.concatenate(
            [
                spread[f * 3 * mid : (f + 1) * 3 * mid, d * cols : (d + brows) * cols]
                for d in range(3)
            ],
            axis=0,
        )

    def stage_block(f, acc):
        kept = first[f, :, cols : (brows + 1) * cols].astype(F32)
        return (acc + wide(c_res, brows) + kept).astype(BF16)

    def stage_time(f, x):
        twice = jnp.dot(wt[:, 2 * mid - x.shape[0] :], x, preferred_element_type=F32)
        live = masks(f, rows * t - 1, brows)
        twice = jnp.where(live, twice + wide(c_time, brows), 0.0).astype(BF16)
        for k in range(2):
            timed[2 * f + k] = twice[k * mid : (k + 1) * mid]

    def stage_up(f):
        x = [timed[f, :, i * cols : (i + rows) * cols] for i in range(3)]
        pairs = [None] * (2 * rows)
        for k in range(2):
            z = jnp.dot(
                wu[k],
                jnp.concatenate([x[k], x[k + 1]], axis=0),
                preferred_element_type=F32,
            )
            for r in range(rows):
                z0, z1, z2 = [
                    z[e * outc : (e + 1) * outc, r * cols : (r + 1) * cols] for e in range(3)
                ]
                live = (f // 2 < n_frames) & (rows * t + r < n_rows)
                base = z1 + c_up[...]
                even = (shift(z0, 1) + z2 + base).astype(BF16)
                odd = (z0 + shift(z2, -1) + base).astype(BF16)
                pair = jnp.concatenate([even, odd], axis=1)
                pairs[2 * r + k] = jnp.where(live, pair, jnp.zeros_like(pair))
        woven = jnp.dot(jnp.concatenate(pairs, axis=0), perm[...], preferred_element_type=F32)
        woven = woven.reshape(2 * rows, outc, 2 * cols)
        result[f] = jnp.transpose(woven, (1, 0, 2)).astype(BF16)
        pltpu.make_async_copy(result.at[f], out_ref.at[0, :, f], sem_o.at[f]).start()


    for p in range(2):
        stage_first(0, p)
    for copy in copies_r + copies_t + [copy_u]:
        copy.wait()
    old = jnp.dot(wr[...], taller(0), preferred_element_type=F32)
    for p in range(2):
        stage_first(1, p)
    w0, w1, w2 = [wu_raw[d].reshape(3 * outc, mid) for d in range(3)]
    wu[0, :, 0:mid] = w0
    wu[0, :, mid:] = (w1.astype(F32) + w2.astype(F32)).astype(BF16)
    wu[1, :, 0:mid] = (w0.astype(F32) + w1.astype(F32)).astype(BF16)
    wu[1, :, mid:] = w2

    block0 = stage_block(0, old[0:mid])
    stage_time(0, block0)
    new = jnp.dot(wr[0:mid], taller(1), preferred_element_type=F32)
    stage_up(0)
    block1 = stage_block(1, old[mid:] + new)
    stage_time(1, jnp.concatenate([block0, block1], axis=0))
    for f in range(1, 2 * LFRAMES):
        stage_up(f)
    for f in range(2 * LFRAMES):
        pltpu.make_async_copy(result.at[f], out_ref.at[0, :, f], sem_o.at[f]).wait()


def decode(grid, frames, heights, widths, w_in, vectors, w_res, w_time, w_up):
    rows, cols = grid.shape[1] - 6, grid.shape[3]
    channels = grid.shape[2]
    mid, outc = w_res.shape[3], w_up.shape[2]
    vmem = pl.BlockSpec(memory_space=pltpu.VMEM)
    return pl.pallas_call(
        decode_kernel,
        out_shape=jax.ShapeDtypeStruct((1, outc, 2 * LFRAMES, 2 * rows, 2 * cols), BF16),
        in_specs=[vmem] + [pl.BlockSpec(memory_space=pltpu.HBM)] * 12,
        out_specs=pl.BlockSpec(memory_space=pltpu.HBM),
        scratch_shapes=[pltpu.SMEM(v.shape, jnp.int32) for v in (frames, heights, widths)]
        + [pltpu.VMEM(v.shape, F32) for v in vectors]
        + [
            pltpu.VMEM((18 * channels, mid), BF16),
            pltpu.VMEM((mid, 18 * channels), BF16),
            pltpu.VMEM((2 * mid, 9 * mid), BF16),
            pltpu.VMEM((2 * mid, 2 * mid), BF16),
            pltpu.VMEM(w_up.shape, BF16),
            pltpu.VMEM((2, 3 * outc, 2 * mid), BF16),
            pltpu.VMEM((18 * channels, (rows + 4) * cols), BF16),
            pltpu.VMEM((LFRAMES, mid, (rows + 4) * cols), BF16),
            pltpu.VMEM((6 * mid, (rows + 4) * cols), BF16),
            pltpu.VMEM((2 * LFRAMES, mid, (rows + 2) * cols), BF16),
            pltpu.VMEM((2 * LFRAMES, outc, 2 * rows, 2 * cols), BF16),
            pltpu.VMEM((2 * cols, 2 * cols), BF16),
            pltpu.VMEM((mid, 128), F32),
            pltpu.VMEM((mid, 128), F32),
            pltpu.VMEM((mid, 128), F32),
            pltpu.VMEM((2 * mid, 128), F32),
            pltpu.VMEM((outc, 128), F32),
            pltpu.SemaphoreType.DMA((3,)),
            pltpu.SemaphoreType.DMA((5,)),
            pltpu.SemaphoreType.DMA((2,)),
            pltpu.SemaphoreType.DMA((3, 6)),
            pltpu.SemaphoreType.DMA((2,)),
            pltpu.SemaphoreType.DMA,
            pltpu.SemaphoreType.DMA((2 * LFRAMES,)),
        ],
        compiler_params=pltpu.CompilerParams(vmem_limit_bytes=VMEM_BYTES),
        name="decode",
    )(grid, frames, heights, widths, w_in, *vectors, w_res, w_time, w_up)


def solution(mesh):
    n_req, n_tile = mesh.shape["req"], mesh.shape["tile"]

    def on_device(
        latents, piece_dest, frames, heights, widths,
        w_in, b_in, gain_norm, w_res, b_res, w_time, b_time, w_up, b_up,
    ):
        grid = route(n_req, n_tile, piece_dest, latents)
        mid, channels = w_in.shape[3], w_in.shape[4]
        taps = jnp.transpose(w_in, (0, 1, 2, 4, 3)).reshape(27 * channels, mid)
        vectors = (b_in, gain_norm, b_res, b_time, b_up)
        return decode(grid, frames, heights, widths, taps, vectors, w_res, w_time, w_up)

    return jax.shard_map(
        on_device,
        mesh=mesh,
        in_specs=(P(("req", "tile"), None, None),) + (P(),) * 13,
        out_specs=P("req", None, None, "tile", None),
        check_vma=False,
    )
```

```python
import functools

import jax
import jax.numpy as jnp
from jax import lax
from jax.experimental import pallas as pl
from jax.experimental.pallas import tpu as pltpu
from jax.sharding import PartitionSpec as P

LFRAMES = 2
MESH = pl.DeviceIdType.MESH
VMEM_BYTES = 63 * 2**20
F32 = jnp.float32
BF16 = jnp.bfloat16


def route_kernel(
    n_req, n_tile, dest_hbm, lat_ref, out_ref,
    dest_ref, held, item, land, dest_sem, send_sem, recv_sem, send_two, recv_two,
):
    g = lax.axis_index("req")
    t = lax.axis_index("tile")
    far = n_req // 2 if n_req < 8 else 4
    low = n_req // far
    line, place = g // low, lax.rem(g, low)
    half = n_tile // 2
    slots = lat_ref.shape[0]
    rows = slots // LFRAMES
    has_up, has_down = t > 0, t < n_tile - 1
    inner = (t + n_tile - 1) // n_tile - (t + 1) // n_tile

    fetch = pltpu.make_async_copy(dest_hbm, dest_ref, dest_sem)
    fetch.start()
    barrier = pltpu.get_barrier_semaphore()

    def greet(group, tile):
        pl.semaphore_signal(barrier, inc=1, device_id=(group, tile), device_id_type=MESH)

    def in_line(k):
        return lax.rem(line + k, far) * low + place

    def in_row(k):
        return line * low + lax.rem(place + k, low)

    for k in range(far):
        for f in range(LFRAMES):
            source = f * half + t // 2
            if k > 0:
                greet(in_line(k), source)
            else:
                pl.when(source != t)(functools.partial(greet, g, source))
    for k in range(low):
        if k > 0:
            greet(in_row(k), t)
        pl.when(has_up)(functools.partial(greet, in_row(k), t - 1))
        pl.when(has_down)(functools.partial(greet, in_row(k), t + 1))

    zeros = jnp.zeros((low, LFRAMES, 3) + lat_ref.shape[1:], BF16)

    @pl.when(t == 0)
    def _():
        land[:, :, 0:3] = zeros

    @pl.when(t == n_tile - 1)
    def _():
        land[:, :, 3 + rows :] = zeros

    pl.semaphore_wait(barrier, 2 * far - 1 + inner + low * (2 + inner) - 1)

    frame = t // half
    first_tile = 2 * lax.rem(t, half)

    def one(k, h):
        return pltpu.make_async_remote_copy(
            src_ref=lat_ref.at[pl.ds(h * rows, rows)],
            dst_ref=held.at[line, frame],
            send_sem=send_sem.at[k, h],
            recv_sem=recv_sem.at[line, frame],
            device_id=(in_line(k), first_tile + h),
            device_id_type=MESH,
        )

    def own(h):
        return pltpu.make_async_copy(
            lat_ref.at[pl.ds(h * rows, rows)], held.at[line, frame], recv_sem.at[line, frame]
        )

    for k in list(range(1, far)) + [0]:
        for h in range(2):
            if k > 0:
                one(k, h).start()
            else:
                pl.when(first_tile + h != t)(lambda h=h: one(0, h).start())
                pl.when(first_tile + h == t)(lambda h=h: own(h).start())

    fetch.wait()
    per = slots * n_tile

    def source_of(group):
        found = jnp.int32(0)
        for j in range(n_req):
            found = jnp.where(dest_ref[j * per] // per == group, j, found)
        return found

    sources = [source_of(in_row(k)) for k in range(low)]

    for s in range(far):
        for f in range(LFRAMES):
            pltpu.make_async_copy(held.at[s, f], held.at[s, f], recv_sem.at[s, f]).wait()

    def two(k, n, src, dst, count, tile):
        return pltpu.make_async_remote_copy(
            src_ref=item.at[k, :, pl.ds(src, count)],
            dst_ref=land.at[place, :, pl.ds(dst, count)],
            send_sem=send_two.at[k, n],
            recv_sem=recv_two.at[place, n],
            device_id=(in_row(k), tile),
            device_id_type=MESH,
        )

    def across(k):
        return two(k, 0, 0, 3, rows, t)

    def up(k):
        return two(k, 1, 0, 3 + rows, 3, t - 1)

    def down(k):
        return two(k, 2, rows - 3, 0, 3, t + 1)

    def keep():
        return pltpu.make_async_copy(
            item.at[0], land.at[place, :, pl.ds(3, rows)], recv_two.at[place, 0]
        )

    for k in list(range(1, low)) + [0]:
        item[k] = held[sources[k] // low]
        if k > 0:
            across(k).start()
        else:
            keep().start()
        pl.when(has_up)(lambda k=k: up(k).start())
        pl.when(has_down)(lambda k=k: down(k).start())

    for k in range(far):
        for h in range(2):
            if k > 0:
                one(k, h).wait_send()
            else:
                pl.when(first_tile + h != t)(lambda h=h: one(0, h).wait_send())

    def landed(p, n, at, count):
        part = land.at[p, :, pl.ds(at, count)]
        pltpu.make_async_copy(part, part, recv_two.at[p, n]).wait()

    for p in range(low):
        landed(p, 0, 3, rows)
        pl.when(has_down)(functools.partial(landed, p, 1, 3 + rows, 3))
        pl.when(has_up)(functools.partial(landed, p, 2, 0, 3))

    out_ref[...] = land[lax.rem(sources[0], low)]

    for k in range(low):
        if k > 0:
            across(k).wait_send()
        pl.when(has_up)(lambda k=k: up(k).wait_send())
        pl.when(has_down)(lambda k=k: down(k).wait_send())


def route(n_req, n_tile, piece_dest, latents):
    slots, channels, cols = latents.shape
    rows = slots // LFRAMES
    far = n_req // 2 if n_req < 8 else 4
    low = n_req // far
    return pl.pallas_call(
        functools.partial(route_kernel, n_req, n_tile),
        out_shape=jax.ShapeDtypeStruct((LFRAMES, rows + 6, channels, cols), BF16),
        in_specs=[pl.BlockSpec(memory_space=pltpu.HBM)] * 2,
        out_specs=pl.BlockSpec(memory_space=pltpu.VMEM),
        scratch_shapes=[
            pltpu.SMEM(piece_dest.shape, jnp.int32),
            pltpu.VMEM((far, LFRAMES, rows, channels, cols), BF16),
            pltpu.VMEM((low, LFRAMES, rows, channels, cols), BF16),
            pltpu.VMEM((low, LFRAMES, rows + 6, channels, cols), BF16),
            pltpu.SemaphoreType.DMA,
            pltpu.SemaphoreType.DMA((far, 2)),
            pltpu.SemaphoreType.DMA((far, LFRAMES)),
            pltpu.SemaphoreType.DMA((low, 3)),
            pltpu.SemaphoreType.DMA((low, 3)),
        ],
        compiler_params=pltpu.CompilerParams(
            collective_id=0, has_side_effects=True, vmem_limit_bytes=VMEM_BYTES
        ),
        name="route",
    )(piece_dest, latents)


def shift(x, by):
    width = x.shape[1]
    lane = lax.broadcasted_iota(jnp.int32, x.shape, 1)
    if by == 1:
        return jnp.where(lane == 0, 0.0, pltpu.roll(x, 1, axis=1))
    return jnp.where(lane == width - 1, 0.0, pltpu.roll(x, width - 1, axis=1))


def column(ref):
    n = ref.shape[0]
    return jnp.transpose(jnp.broadcast_to(ref[...].reshape(1, n), (128, n)))


def decode_kernel(grid_ref, *refs):
    hbm, (out_ref, *refs) = refs[:12], refs[12:]
    frames_hbm, heights_hbm, widths_hbm, w_in_hbm = hbm[:4]
    vector_hbm, (w_res_hbm, w_time_hbm, w_up_hbm) = hbm[4:9], hbm[9:]
    frames_ref, heights_ref, widths_ref, *refs = refs
    vectors, refs = refs[:5], refs[5:]
    taps, w_in, wr, wt, wu_raw, wu, x_in, first, spread, timed, result, perm, *refs = refs
    c_in, c_gain, c_res, c_time, c_up, sem_s, sem_v, sem_i, sem_r, sem_t, sem_u, sem_o = refs
    g = lax.axis_index("req")
    t = lax.axis_index("tile")
    channels, cols = grid_ref.shape[2], grid_ref.shape[3]
    rows = grid_ref.shape[1] - 6
    mid = taps.shape[1]
    outc = wu_raw.shape[2]
    one = 9 * channels
    mrows = rows + 4

    copies_s = [
        pltpu.make_async_copy(a, b, sem_s.at[i])
        for i, (a, b) in enumerate(
            zip((frames_hbm, heights_hbm, widths_hbm), (frames_ref, heights_ref, widths_ref))
        )
    ]
    copies_v = [
        pltpu.make_async_copy(a, b, sem_v.at[i])
        for i, (a, b) in enumerate(zip(vector_hbm, vectors))
    ]
    copies_i = [
        pltpu.make_async_copy(
            w_in_hbm.at[pl.ds((2 - i) * one, one)], taps.at[pl.ds(i * one, one)], sem_i.at[i]
        )
        for i in range(2)
    ]
    copies_r = []
    for d in range(3):
        for a in range(2):
            for e in range(3):
                copies_r.append(
                    pltpu.make_async_copy(
                        w_res_hbm.at[2 - a, d, e],
                        wr.at[pl.ds(a * mid, mid), pl.ds((d * 3 + e) * mid, mid)],
                        sem_r.at[d, a * 3 + e],
                    )
                )
    copies_t = [
        pltpu.make_async_copy(w_time_hbm.at[a + 1], wt.at[:, pl.ds(a * mid, mid)], sem_t.at[a])
        for a in range(2)
    ]
    copy_u = pltpu.make_async_copy(w_up_hbm, wu_raw, sem_u)
    for copy in copies_s + copies_v + copies_i + copies_r + copies_t + [copy_u]:
        copy.start()

    for copy in copies_s:
        copy.wait()
    n_frames, n_rows, n_cols = frames_ref[g], heights_ref[g], widths_ref[g]
    lane = lax.broadcasted_iota(jnp.int32, (1, cols), 1)

    def mask(f, r):
        live = (f < n_frames) & (r >= 0) & (r < n_rows)
        return lane < jnp.where(live, n_cols, 0)

    src = lax.broadcasted_iota(jnp.int32, (2 * cols, 2 * cols), 0)
    dst = lax.broadcasted_iota(jnp.int32, (2 * cols, 2 * cols), 1)
    pick = (src % cols == dst // 2) & (src // cols == dst % 2) & (dst // 2 < n_cols)
    perm[...] = jnp.where(pick, 1.0, 0.0).astype(BF16)

    def masks(f, r, n):
        return jnp.concatenate([mask(f, r + i) for i in range(n)], axis=1)

    def wide(ref, n):
        return jnp.concatenate([ref[...]] * n, axis=1)

    for f in range(LFRAMES):
        base = (1 - f) * one
        for q in range(rows + 6):
            x = grid_ref[f, q].astype(F32)
            x = jnp.where(mask(f, rows * t - 3 + q), x, 0.0)
            for e, y in enumerate((shift(x, 1), x, shift(x, -1))):
                y = y.astype(BF16)
                for d in range(3):
                    if 0 <= q - d < mrows:
                        at = base + (d * 3 + e) * channels
                        x_in[at : at + channels, (q - d) * cols : (q - d + 1) * cols] = y

    for copy in copies_v + copies_i:
        copy.wait()
    w_in[...] = jnp.transpose(taps[...])
    for kept, vector in zip((c_in, c_gain, c_res, c_time, c_up), vectors):
        kept[...] = column(vector)

    span = mrows // 2

    def stage_first(f, p):
        at = p * span * cols
        here = pl.ds(at, span * cols)
        x = x_in[one : 2 * one, here] if f == 0 else x_in[:, here]
        acc = jnp.dot(w_in[:, 0 : x.shape[0]], x, preferred_element_type=F32)
        half = (acc + wide(c_in, span)).astype(BF16)
        first[f, :, here] = half
        v = half.astype(F32)
        mean = jnp.sum(v * v, axis=0, keepdims=True) * (1.0 / mid)
        v = v * lax.rsqrt(mean + 1e-06) * wide(c_gain, span)
        v = 0.5 * v * (1.0 + jnp.tanh(0.5 * v))
        v = jnp.where(masks(f, rows * t - 2 + span * p, span), v, 0.0)
        parts = [v[:, i * cols : (i + 1) * cols] for i in range(span)]
        for e in range(3):
            moved = parts if e == 1 else [shift(part, 1 - e) for part in parts]
            spread[(f * 3 + e) * mid : (f * 3 + e + 1) * mid, here] = jnp.concatenate(
                moved, axis=1
            ).astype(BF16)

    brows = rows + 2

    def taller(f):
        return jnp.concatenate(
            [
                spread[f * 3 * mid : (f + 1) * 3 * mid, d * cols : (d + brows) * cols]
                for d in range(3)
            ],
            axis=0,
        )

    def stage_block(f, acc):
        kept = first[f, :, cols : (brows + 1) * cols].astype(F32)
        return (acc + wide(c_res, brows) + kept).astype(BF16)

    def stage_time(f, x):
        twice = jnp.dot(wt[:, 2 * mid - x.shape[0] :], x, preferred_element_type=F32)
        live = masks(f, rows * t - 1, brows)
        twice = jnp.where(live, twice + wide(c_time, brows), 0.0).astype(BF16)
        for k in range(2):
            timed[2 * f + k] = twice[k * mid : (k + 1) * mid]

    def stage_up(f):
        x = [timed[f, :, i * cols : (i + rows) * cols] for i in range(3)]
        pairs = [None] * (2 * rows)
        for k in range(2):
            z = jnp.dot(
                wu[k],
                jnp.concatenate([x[k], x[k + 1]], axis=0),
                preferred_element_type=F32,
            )
            for r in range(rows):
                z0, z1, z2 = [
                    z[e * outc : (e + 1) * outc, r * cols : (r + 1) * cols] for e in range(3)
                ]
                live = (f // 2 < n_frames) & (rows * t + r < n_rows)
                base = z1 + c_up[...]
                even = (shift(z0, 1) + z2 + base).astype(BF16)
                odd = (z0 + shift(z2, -1) + base).astype(BF16)
                pair = jnp.concatenate([even, odd], axis=1)
                pairs[2 * r + k] = jnp.where(live, pair, jnp.zeros_like(pair))
        woven = jnp.dot(jnp.concatenate(pairs, axis=0), perm[...], preferred_element_type=F32)
        woven = woven.reshape(2 * rows, outc, 2 * cols)
        result[f] = jnp.transpose(woven, (1, 0, 2)).astype(BF16)
        pltpu.make_async_copy(result.at[f], out_ref.at[0, :, f], sem_o.at[f]).start()


    for p in range(2):
        stage_first(0, p)
    for copy in copies_r:
        copy.wait()
    old = jnp.dot(wr[...], taller(0), preferred_element_type=F32)
    for p in range(2):
        stage_first(1, p)
    for copy in copies_t + [copy_u]:
        copy.wait()
    w0, w1, w2 = [wu_raw[d].reshape(3 * outc, mid) for d in range(3)]
    wu[0, :, 0:mid] = w0
    wu[0, :, mid:] = (w1.astype(F32) + w2.astype(F32)).astype(BF16)
    wu[1, :, 0:mid] = (w0.astype(F32) + w1.astype(F32)).astype(BF16)
    wu[1, :, mid:] = w2

    block0 = stage_block(0, old[0:mid])
    stage_time(0, block0)
    new = jnp.dot(wr[0:mid], taller(1), preferred_element_type=F32)
    stage_up(0)
    block1 = stage_block(1, old[mid:] + new)
    stage_time(1, jnp.concatenate([block0, block1], axis=0))
    for f in range(1, 2 * LFRAMES):
        stage_up(f)
    for f in range(2 * LFRAMES):
        pltpu.make_async_copy(result.at[f], out_ref.at[0, :, f], sem_o.at[f]).wait()


def decode(grid, frames, heights, widths, w_in, vectors, w_res, w_time, w_up):
    rows, cols = grid.shape[1] - 6, grid.shape[3]
    channels = grid.shape[2]
    mid, outc = w_res.shape[3], w_up.shape[2]
    vmem = pl.BlockSpec(memory_space=pltpu.VMEM)
    return pl.pallas_call(
        decode_kernel,
        out_shape=jax.ShapeDtypeStruct((1, outc, 2 * LFRAMES, 2 * rows, 2 * cols), BF16),
        in_specs=[vmem] + [pl.BlockSpec(memory_space=pltpu.HBM)] * 12,
        out_specs=pl.BlockSpec(memory_space=pltpu.HBM),
        scratch_shapes=[pltpu.SMEM(v.shape, jnp.int32) for v in (frames, heights, widths)]
        + [pltpu.VMEM(v.shape, F32) for v in vectors]
        + [
            pltpu.VMEM((18 * channels, mid), BF16),
            pltpu.VMEM((mid, 18 * channels), BF16),
            pltpu.VMEM((2 * mid, 9 * mid), BF16),
            pltpu.VMEM((2 * mid, 2 * mid), BF16),
            pltpu.VMEM(w_up.shape, BF16),
            pltpu.VMEM((2, 3 * outc, 2 * mid), BF16),
            pltpu.VMEM((18 * channels, (rows + 4) * cols), BF16),
            pltpu.VMEM((LFRAMES, mid, (rows + 4) * cols), BF16),
            pltpu.VMEM((6 * mid, (rows + 4) * cols), BF16),
            pltpu.VMEM((2 * LFRAMES, mid, (rows + 2) * cols), BF16),
            pltpu.VMEM((2 * LFRAMES, outc, 2 * rows, 2 * cols), BF16),
            pltpu.VMEM((2 * cols, 2 * cols), BF16),
            pltpu.VMEM((mid, 128), F32),
            pltpu.VMEM((mid, 128), F32),
            pltpu.VMEM((mid, 128), F32),
            pltpu.VMEM((2 * mid, 128), F32),
            pltpu.VMEM((outc, 128), F32),
            pltpu.SemaphoreType.DMA((3,)),
            pltpu.SemaphoreType.DMA((5,)),
            pltpu.SemaphoreType.DMA((2,)),
            pltpu.SemaphoreType.DMA((3, 6)),
            pltpu.SemaphoreType.DMA((2,)),
            pltpu.SemaphoreType.DMA,
            pltpu.SemaphoreType.DMA((2 * LFRAMES,)),
        ],
        compiler_params=pltpu.CompilerParams(vmem_limit_bytes=VMEM_BYTES),
        name="decode",
    )(grid, frames, heights, widths, w_in, *vectors, w_res, w_time, w_up)


def solution(mesh):
    n_req, n_tile = mesh.shape["req"], mesh.shape["tile"]

    def on_device(
        latents, piece_dest, frames, heights, widths,
        w_in, b_in, gain_norm, w_res, b_res, w_time, b_time, w_up, b_up,
    ):
        grid = route(n_req, n_tile, piece_dest, latents)
        mid, channels = w_in.shape[3], w_in.shape[4]
        taps = jnp.transpose(w_in, (0, 1, 2, 4, 3)).reshape(27 * channels, mid)
        vectors = (b_in, gain_norm, b_res, b_time, b_up)
        return decode(grid, frames, heights, widths, taps, vectors, w_res, w_time, w_up)

    return jax.shard_map(
        on_device,
        mesh=mesh,
        in_specs=(P(("req", "tile"), None, None),) + (P(),) * 13,
        out_specs=P("req", None, None, "tile", None),
        check_vma=False,
    )
```
